256 devices in a mesh: dp: 16 (over z_hi, x, core), tensor: 16 (over y, z_lo).
Axes of the slice: x: 4, y: 4, z: 8 (z_hi: 2, z_lo: 4; z = z_hi * 4 + z_lo), core: 2. Of those that a mesh axis runs over, the one named last changes fastest.
Arguments:
- q_nope: bfloat16 [2, 512, 64, 128], P(None, ('dp', 'tensor')), may hold values from -6 to 6
- q_rope: bfloat16 [2, 512, 64, 64], P(None, ('dp', 'tensor')), may hold values from -64 to 64
- cache_latent: bfloat16 [512, 2048, 512], P(('dp', 'tensor')), may hold values from -6 to 6
- cache_rope: bfloat16 [512, 64, 2048], P(('dp', 'tensor')), may hold values from -6 to 6
- cache_len: int32 [512], P(('dp', 'tensor')), may hold values from 2 to 2048, as said below
- new_latent: bfloat16 [2, 512, 512], P(None, ('dp', 'tensor')), may hold values from -6 to 6
- new_rope: bfloat16 [2, 512, 64], P(None, ('dp', 'tensor')), may hold values from -6 to 6
- slot_request: int32 [512], replicated, may hold values from 0 to 511, each once
- w_uk: bfloat16 [64, 128, 512], P('tensor'), may hold values from -0.5 to 0.5
- w_uv: bfloat16 [64, 512, 128], P('tensor'), may hold values from -0.25 to 0.25
- w_out: bfloat16 [8192, 7168], P('tensor', 'dp'), may hold values from -0.5 to 0.5
- hidden_state: bfloat16 [2, 512, 7168], P(None, 'tensor', 'dp'), may hold values from -64 to 64
- norm_gain: bfloat16 [7168], P('dp'), may hold values from 0.5 to 1.5
- w_gate: bfloat16 [7168, 18432], P('dp', 'tensor'), may hold values from -0.0625 to 0.0625
- w_up: bfloat16 [7168, 18432], P('dp', 'tensor'), may hold values from -0.0625 to 0.0625
- w_down: bfloat16 [18432, 7168], P('tensor', 'dp'), may hold values from -0.046875 to 0.046875
Outputs:
- layer_out: bfloat16 [2, 512, 7168], P(None, 'tensor', 'dp')
The draws below stay inside these ranges and needn't reach their ends.
Inputs may be any that keep to these rules, and one draw needn't show every extreme that they name: A request slot's cache holds valid positions 0 to cache_len - 1; in every draw some slot is full. `slot_request`: each request is served by exactly one slot.
All inputs are finite; a program needn't handle non-finite values.
Results may differ from the reference program's by a relative error of at most 0.024.
Values may be sent and summed in bfloat16 or wider, within the bound.
A program may use at most 128 MiB of HBM per device.

```python
import math
import jax
import jax.numpy as jnp
from jax import lax

D = 7168
H = 64
NOPE = 128
ROPE = 64
LAT = 512
V = 128
FF = 18432
L = 2048
S = 2
R = 512
N_DP = 16


def draw_cache_rope(key, part):
    key = jax.random.fold_in(key, 11)
    base = jnp.clip(jax.random.normal(key, (R, ROPE, L), jnp.float32), -6.0, 6.0)
    return base.astype(jnp.bfloat16)


def draw_q_rope(key, part):
    key = jax.random.fold_in(key, 12)
    base = jnp.clip(jax.random.normal(key, (S, R, H, ROPE), jnp.float32), -6.0, 6.0)
    return base.astype(jnp.bfloat16)


def draw_cache_len(key, part):
    key = jax.random.fold_in(key, 13)
    keys = jax.random.split(key, 2)
    lengths = jax.random.randint(keys[0], (R,), 2, L + 1, jnp.int32)
    full_slot = jax.random.randint(keys[1], (), 0, R, jnp.int32)
    return lengths.at[full_slot].set(L)


def draw_hidden_state(key, part):
    key = jax.random.fold_in(key, 14)
    keys = jax.random.split(key, 2)
    column = jnp.arange(D, dtype=jnp.float32) / D
    base = jnp.clip(jax.random.normal(keys[0], (S, R, D), jnp.float32), -6.0, 6.0)
    column_scale = 0.2 * jnp.power(10.0, column)
    row_scale = jnp.exp(jax.random.uniform(keys[1], (R,), jnp.float32, math.log(0.5), math.log(5.0)))
    return (base * column_scale[None, None, :] * row_scale[None, :, None]).astype(jnp.bfloat16)


def shard_levels(own_key, shape, cuts, least, top_value):
    loudness = 1.0
    for dim, shards_of in cuts:
        draws = jax.random.uniform(jax.random.fold_in(jax.random.fold_in(own_key, 6), dim), (shards_of,), jnp.float32, least / len(cuts), top_value / len(cuts))
        loudness = loudness * jnp.repeat(jnp.exp(draws), shape[dim] // shards_of).reshape((-1,) + (1,) * (len(shape) - 1 - dim))
    return loudness


def normal_values(key, dims, spread, most, shards=(), kind=jnp.bfloat16):
    values = spread * jax.random.normal(key, dims, jnp.float32)
    if shards:
        values = values * shard_levels(key, dims, shards, -0.22, 0.18)
    return jnp.clip(values, -most, most).astype(kind)


def setup_inputs(seed: int = 0) -> dict:
    arg_keys = jax.random.split(jax.random.key(seed), 17)
    return {
        "q_nope": normal_values(arg_keys[0], (S, R, H, NOPE), 1.0, 6.0, ((1, 256),)),
        "q_rope": draw_q_rope(jax.random.fold_in(arg_keys[16], 71), 0),
        "cache_latent": normal_values(arg_keys[2], (R, L, LAT), 1.0, 6.0, ((0, 256),)),
        "cache_rope": draw_cache_rope(jax.random.fold_in(arg_keys[16], 71), 0),
        "cache_len": draw_cache_len(jax.random.fold_in(arg_keys[16], 71), 0),
        "new_latent": normal_values(arg_keys[5], (S, R, LAT), 1.0, 6.0, ((1, 256),)),
        "new_rope": normal_values(arg_keys[6], (S, R, ROPE), 1.0, 6.0, ((1, 256),)),
        "slot_request": jax.random.permutation(arg_keys[7], R).astype(jnp.int32),
        "w_uk": normal_values(arg_keys[8], (H, NOPE, LAT), NOPE ** -0.5, 0.5, ((0, 16),)),
        "w_uv": normal_values(arg_keys[9], (H, LAT, V), LAT ** -0.5, 0.25, ((0, 16),)),
        "w_out": normal_values(arg_keys[10], (H * V, D), V ** -0.5, 0.5, ((0, 16), (1, 16))),
        "hidden_state": draw_hidden_state(jax.random.fold_in(arg_keys[16], 71), 0),
        "norm_gain": jnp.clip(1.0 + 0.1 * jax.random.normal(arg_keys[12], (D,), jnp.float32), 0.5, 1.5).astype(jnp.bfloat16),
        "w_gate": normal_values(arg_keys[13], (D, FF), D ** -0.5, 0.0625, ((0, 16), (1, 16))),
        "w_up": normal_values(arg_keys[14], (D, FF), D ** -0.5, 0.0625, ((0, 16), (1, 16))),
        "w_down": normal_values(arg_keys[15], (FF, D), FF ** -0.5, 0.046875, ((0, 16), (1, 16))),
    }


def row_attend(items):
    q_lat, q_rot, cache_lat, cache_rot, length, new_lat, new_rot = items
    scale = 1.0 / math.sqrt(NOPE + ROPE)
    cache_scores = jnp.einsum('shc,pc->shp', q_lat.astype(jnp.float32), cache_lat.astype(jnp.float32))
    cache_scores = cache_scores + jnp.einsum('she,ep->shp', q_rot.astype(jnp.float32), cache_rot.astype(jnp.float32))
    cache_scores = cache_scores * scale
    valid = (jnp.arange(L, dtype=jnp.int32) < length)[None, None, :]
    cache_scores = jnp.where(valid, cache_scores, -1e+30)
    new_scores = jnp.einsum('shc,uc->shu', q_lat.astype(jnp.float32), new_lat.astype(jnp.float32))
    new_scores = new_scores + jnp.einsum('she,ue->shu', q_rot.astype(jnp.float32), new_rot.astype(jnp.float32))
    new_scores = new_scores * scale
    steps_here = jnp.arange(S, dtype=jnp.int32)
    new_valid = (steps_here[None, :] <= steps_here[:, None])[:, None, :]
    new_scores = jnp.where(new_valid, new_scores, -1e+30)
    top = jnp.maximum(lax.optimization_barrier(jnp.max(cache_scores, axis=-1)), lax.optimization_barrier(jnp.max(new_scores, axis=-1)))
    cache_exp = jnp.where(valid, jnp.exp(cache_scores - top[..., None]), 0.0)
    new_exp = jnp.where(new_valid, jnp.exp(new_scores - top[..., None]), 0.0)
    total = lax.optimization_barrier(jnp.sum(cache_exp, axis=-1)) + lax.optimization_barrier(jnp.sum(new_exp, axis=-1))
    cache_probs = (cache_exp / total[..., None]).astype(jnp.bfloat16)
    new_probs = (new_exp / total[..., None]).astype(jnp.bfloat16)
    result = jnp.einsum('shp,pc->shc', cache_probs.astype(jnp.float32), cache_lat.astype(jnp.float32))
    result = result + jnp.einsum('shu,uc->shc', new_probs.astype(jnp.float32), new_lat.astype(jnp.float32))
    return result.astype(jnp.bfloat16)

def reference(q_nope, q_rope, cache_latent, cache_rope, cache_len, new_latent, new_rope, slot_request, w_uk, w_uv, w_out, hidden_state, norm_gain, w_gate, w_up, w_down):
    q_latent = jnp.einsum('srhn,hnc->srhc', q_nope.astype(jnp.float32), w_uk.astype(jnp.float32)).astype(jnp.bfloat16)
    items = (jnp.moveaxis(q_latent, 1, 0), jnp.moveaxis(q_rope, 1, 0), cache_latent, cache_rope, cache_len, jnp.moveaxis(new_latent, 1, 0), jnp.moveaxis(new_rope, 1, 0))
    out_latent = jnp.moveaxis(lax.map(row_attend, items), 0, 1)
    head_out = jnp.einsum('srhc,hcv->srhv', out_latent.astype(jnp.float32), w_uv.astype(jnp.float32)).astype(jnp.bfloat16)
    head_out = head_out.reshape(S, R, H * V)
    inverse = jnp.argsort(slot_request).astype(jnp.int32)
    attn_rows = jnp.take(head_out, inverse, axis=1)
    projected = jnp.dot(attn_rows.reshape(S * R, H * V), w_out, preferred_element_type=jnp.float32).reshape(S, R, D)
    after_attn = (hidden_state.astype(jnp.float32) + projected).astype(jnp.bfloat16)
    wide = after_attn.astype(jnp.float32)
    mean_sq = lax.optimization_barrier(jnp.mean(wide * wide, axis=-1, keepdims=True))
    normed = (wide * lax.rsqrt(mean_sq + 1e-06) * norm_gain.astype(jnp.float32)).astype(jnp.bfloat16)
    flat = normed.reshape(S * R, D)
    block = D // N_DP

    def add_block(index, carry):
        gate_sum, up_sum = carry
        begin = (index * block).astype(jnp.int32)
        piece = lax.dynamic_slice_in_dim(flat, begin, block, 1)
        gate_part = jnp.dot(piece, lax.dynamic_slice_in_dim(w_gate, begin, block, 0), preferred_element_type=jnp.float32)
        up_part = jnp.dot(piece, lax.dynamic_slice_in_dim(w_up, begin, block, 0), preferred_element_type=jnp.float32)
        gate_part = lax.optimization_barrier(gate_part.astype(jnp.bfloat16)).astype(jnp.float32)
        up_part = lax.optimization_barrier(up_part.astype(jnp.bfloat16)).astype(jnp.float32)
        return (gate_sum + gate_part, up_sum + up_part)
    zeros = jnp.zeros((S * R, FF), jnp.float32)
    gate, up = lax.fori_loop(jnp.int32(0), jnp.int32(N_DP), add_block, (zeros, zeros))
    act = (jax.nn.silu(gate) * up).astype(jnp.bfloat16)
    down = jnp.dot(act, w_down, preferred_element_type=jnp.float32).reshape(S, R, D)
    return (after_attn.astype(jnp.float32) + down).astype(jnp.bfloat16)
```

```python
import jax
import jax.numpy as jnp
from jax import lax
from jax.experimental import pallas as pl
from jax.experimental.pallas import tpu as pltpu
from jax.sharding import PartitionSpec as P

D = 7168
MESH = pl.DeviceIdType.MESH
BF = jnp.bfloat16
F32 = jnp.float32


def dot(a, b):
    return jnp.dot(a, b, preferred_element_type=F32)


def dot_nt(a, b):
    return lax.dot_general(a, b, (((1,), (1,)), ((), ())), preferred_element_type=F32)


def iota(shape, dim):
    return lax.broadcasted_iota(jnp.int32, shape, dim)


def layer_kernel(
    q_ref,
    q_rot_ref,
    len_ref,
    new_lat_ref,
    new_rot_ref,
    slot_ref,
    gain_ref,
    hidden_ref,
    lat_hbm,
    rot_hbm,
    uk_hbm,
    uv_hbm,
    out_hbm,
    gate_hbm,
    up_hbm,
    down_hbm,
    o_ref,
    q_recv,
    ql_send,
    ql_recv,
    ol_send,
    ol_recv,
    lat,
    rot,
    uk,
    uv,
    w_out,
    w_down,
    w_in,
    w_mix,
    gains,
    perm,
    heads,
    part,
    part_y,
    part_mid,
    part_z,
    after,
    x_all,
    y_part,
    y_recv,
    s_part,
    s_recv,
    y_mid,
    y_last,
    s_last,
    acts,
    down_part,
    down_y,
    down_mid,
    down_z,
    local_sem,
    send_sem,
    recv_sem,
):
    d = lax.axis_index("dp")
    t = lax.axis_index("tensor")
    zh = lax.div(d, 8)
    x = lax.rem(lax.div(d, 2), 4)
    c = lax.rem(d, 2)
    y = lax.div(t, 4)
    zl = lax.rem(t, 4)
    other = 1 - c
    sibling = (d + 1 - 2 * c, t)
    z_partner = (lax.rem(d + 8, 16), t)

    def along_x(k):
        return (zh * 8 + lax.rem(x + k + 4, 4) * 2 + c, t)

    def along_y(k):
        return (d, lax.rem(y + k + 4, 4) * 4 + zl)

    def along_z(k):
        return (d, y * 4 + lax.rem(zl + k + 4, 4))

    sent = []

    def remote(src, dst, phase, i, device):
        return pltpu.make_async_remote_copy(
            src_ref=src,
            dst_ref=dst,
            send_sem=send_sem.at[phase, i],
            recv_sem=recv_sem.at[phase, i],
            device_id=device,
            device_id_type=MESH,
        )

    def send(src, dst, phase, i, device):
        copy = remote(src, dst, phase, i, device)
        copy.start()
        sent.append(copy)

    def arrived(dst, phase, i, device):
        remote(dst, dst, phase, i, device).wait_recv()

    def load(src, dst, i):
        copy = pltpu.make_async_copy(src, dst, local_sem.at[i])
        copy.start()
        return copy

    load_uk = load(uk_hbm, uk, 0)
    load_lat = load(lat_hbm, lat, 1)
    load_rot = load(rot_hbm, rot, 2)
    load_uv = load(uv_hbm, uv, 3)
    load_out = load(out_hbm, w_out, 4)
    mine = pl.ds(pl.multiple_of(c * 512, 512), 512)
    load_in = [
        load(gate_hbm.at[:, mine], w_in.at[c, :, pl.ds(0, 512)], 5),
        load(up_hbm.at[:, mine], w_in.at[c, :, pl.ds(512, 512)], 6),
        load(gate_hbm.at[:, pl.ds(1024, 128)], w_in.at[c, :, pl.ds(1024, 128)], 7),
        load(up_hbm.at[:, pl.ds(1024, 128)], w_in.at[c, :, pl.ds(1152, 128)], 8),
        load(gain_ref, gains.at[c], 9),
    ]
    load_down = load(down_hbm, w_down, 10)

    barrier = pltpu.get_barrier_semaphore()

    def greet(i, carry):
        pl.semaphore_signal(
            barrier, inc=1, device_id=(d, lax.rem(t + i, 16)), device_id_type=MESH
        )
        return carry

    lax.fori_loop(1, 16, greet, 0)
    for device in (z_partner, along_x(1), along_x(2), along_x(3), sibling):
        pl.semaphore_signal(barrier, inc=1, device_id=device, device_id_type=MESH)
    pl.semaphore_wait(barrier, 20)

    def exchange_start(src, dst, phase):
        def one(i, carry):
            p = lax.rem(t + i, 16)
            remote(src.at[p], dst.at[t], phase, i, (d, p)).start()
            return carry

        lax.fori_loop(1, 16, one, 0)
        dst[t] = src[t]

    def exchange_wait(src, dst, phase):
        def one(i, carry):
            p = lax.rem(t + 16 - i, 16)
            remote(src.at[p], dst.at[p], phase, i, (d, p)).wait_recv()
            return carry

        lax.fori_loop(1, 16, one, 0)

    def exchange_end(src, dst, phase):
        def one(i, carry):
            p = lax.rem(t + i, 16)
            remote(src.at[p], dst.at[t], phase, i, (d, p)).wait_send()
            return carry

        lax.fori_loop(1, 16, one, 0)

    exchange_start(q_ref, q_recv, 0)

    theirs = pl.ds(pl.multiple_of(other * 512, 512), 512)
    send(gate_hbm.at[:, theirs], w_in.at[c, :, pl.ds(0, 512)], 1, 0, sibling)
    send(up_hbm.at[:, theirs], w_in.at[c, :, pl.ds(512, 512)], 1, 1, sibling)
    send(gate_hbm.at[:, pl.ds(1024, 128)], w_in.at[c, :, pl.ds(1024, 128)], 1, 2, sibling)
    send(up_hbm.at[:, pl.ds(1024, 128)], w_in.at[c, :, pl.ds(1152, 128)], 1, 3, sibling)
    send(gain_ref, gains.at[c], 1, 4, sibling)

    load_uk.wait()
    exchange_wait(q_ref, q_recv, 0)
    head_of_row = lax.div(lax.rem(iota((256, 512), 0), 8), 2)
    q_rows = q_recv[...].reshape(256, 128)
    q_lat = jnp.zeros((256, 512), F32)
    for j in range(4):
        q_lat = jnp.where(head_of_row == j, dot(q_rows, uk[j]), q_lat)
    ql_send[...] = q_lat.astype(BF).reshape(16, 16, 512)
    exchange_start(ql_send, ql_recv, 2)

    request = slot_ref[...]
    perm[...] = jnp.where(iota((512, 512), 0) == request, 1.0, 0.0).astype(BF)
    for copy in load_in:
        copy.wait()
    arrived(w_in.at[other, :, pl.ds(0, 512)], 1, 0, sibling)
    arrived(w_in.at[other, :, pl.ds(512, 512)], 1, 1, sibling)
    arrived(w_in.at[other, :, pl.ds(1024, 128)], 1, 2, sibling)
    arrived(w_in.at[other, :, pl.ds(1152, 128)], 1, 3, sibling)
    arrived(gains.at[other], 1, 4, sibling)
    low = iota((448, 128), 1) < 64
    for k in range(2):
        gain = gains[k].astype(F32)
        for j in range(8):
            cols = pl.ds(j * 128, 128)
            w_mix[k, :, cols] = (w_in[k, :, cols].astype(F32) * gain).astype(BF)
        gate_tail = w_in[k, :, pl.ds(1024, 128)].astype(F32)
        up_tail = w_in[k, :, pl.ds(1152, 128)].astype(F32)
        first = jnp.where(low, gate_tail, pltpu.roll(up_tail, 64, 1))
        second = jnp.where(low, pltpu.roll(gate_tail, 64, 1), up_tail)
        tail = jnp.where(c == 0, first, second)
        w_mix[k, :, pl.ds(1024, 128)] = (tail * gain).astype(BF)

    load_lat.wait()
    load_rot.wait()
    exchange_wait(ql_send, ql_recv, 2)
    scale = 1.0 / 192.0**0.5
    step = lax.rem(iota((128, 1), 0), 2)
    q_all = ql_recv[...].astype(F32)
    results = []
    for r in range(2):
        q_wide = q_all[:, 8 * r : 8 * r + 8, :].reshape(128, 512)
        q = q_wide.astype(BF)
        q_rot = q_rot_ref[r]
        scores = (dot_nt(q, lat[r]) + dot(q_rot, rot[r])) * scale
        scores = jnp.where(iota((128, 2048), 1) < len_ref[r], scores, -1e30)
        q_rot_wide = q_rot.astype(F32)
        top = jnp.max(scores, axis=1, keepdims=True)
        fresh = []
        for u in range(2):
            value = jnp.sum(q_wide * new_lat_ref[u, r : r + 1, :].astype(F32), axis=1, keepdims=True)
            value = value + jnp.sum(
                q_rot_wide * new_rot_ref[u, r : r + 1, :].astype(F32), axis=1, keepdims=True
            )
            value = jnp.where(step >= u, value * scale, -1e30)
            top = jnp.maximum(top, value)
            fresh.append(value)
        weights = jnp.exp(scores - top)
        total = jnp.sum(weights, axis=1, keepdims=True)
        mixed = dot(weights.astype(BF), lat[r])
        for u in range(2):
            weight = jnp.exp(fresh[u] - top)
            total = total + weight
            mixed = mixed + weight * new_lat_ref[u, r : r + 1, :].astype(F32)
        results.append((mixed / total).reshape(16, 8, 512))
    ol_send[...] = jnp.concatenate(results, axis=1).astype(BF)

    exchange_start(ol_send, ol_recv, 3)
    load_uv.wait()
    load_out.wait()
    row = iota((64, 256), 0)
    col = iota((64, 256), 1)
    pick = (
        (lax.div(row, 32) == lax.rem(col, 2))
        & (lax.div(lax.rem(row, 32), 2) == lax.div(col, 16))
        & (lax.rem(row, 2) == lax.rem(lax.div(col, 8), 2))
    )
    pick = jnp.where(pick, 1.0, 0.0).astype(BF)
    exchange_wait(ol_send, ol_recv, 3)
    o_rows = ol_recv[...].reshape(256, 512)
    own_head = lax.div(lax.rem(iota((256, 128), 0), 8), 2)
    spread = [jnp.where(own_head == j, dot(o_rows, uv[j]), 0.0).astype(BF) for j in range(4)]
    block = x * 2 + zh
    heads[c, block] = dot(pick, jnp.concatenate(spread, axis=1)).astype(BF)

    def gather_dp(buf, phase):
        def to_sibling(b, i):
            send(buf.at[c, b], buf.at[c, b], phase, 8 + i, sibling)

        far = x * 2 + 1 - zh
        send(buf.at[c, block], buf.at[c, block], phase, 0, z_partner)
        for k in (2, 1, 3):
            send(buf.at[c, block], buf.at[c, block], phase, k, along_x(k))
        to_sibling(block, 0)
        arrived(buf.at[c, far], phase, 0, z_partner)
        for k in (2, 1, 3):
            send(buf.at[c, far], buf.at[c, far], phase, 4 + k, along_x(k))
        to_sibling(far, 1)
        for k in (1, 3, 2):
            from_x = lax.rem(x - k + 4, 4) * 2
            arrived(buf.at[c, from_x + zh], phase, k, along_x(-k))
            to_sibling(from_x + zh, 1 + k)
        for k in (1, 3, 2):
            from_x = lax.rem(x - k + 4, 4) * 2
            arrived(buf.at[c, from_x + 1 - zh], phase, 4 + k, along_x(-k))
            to_sibling(from_x + 1 - zh, 4 + k)
        arrived(buf.at[other, block], phase, 8, sibling)
        arrived(buf.at[other, far], phase, 9, sibling)
        for k in (1, 3, 2):
            from_x = lax.rem(x - k + 4, 4) * 2
            arrived(buf.at[other, from_x + zh], phase, 9 + k, sibling)
            arrived(buf.at[other, from_x + 1 - zh], phase, 12 + k, sibling)

    def scatter_tensor(chunk, buf, from_y, mid, from_z, phase):
        for k in (2, 1, 3, 0):
            j = lax.rem(y + k, 4)
            chunk(j)
            if k:
                send(buf.at[pl.ds(4 * j, 4)], from_y.at[k - 1], phase, k, along_y(k))
        for k in (1, 3, 2):
            arrived(from_y.at[k - 1], phase, k, along_y(-k))
        total = buf[pl.ds(4 * y, 4)].astype(F32)
        for k in (1, 3, 2):
            total = total + from_y[k - 1].astype(F32)
        mid[...] = total.astype(BF)
        for k in (2, 1, 3):
            send(mid.at[lax.rem(zl + k, 4)], from_z.at[k - 1], phase, 4 + k, along_z(k))
        total = mid[zl].astype(F32)
        for k in (1, 3, 2):
            arrived(from_z.at[k - 1], phase, 4 + k, along_z(-k))
            total = total + from_z[k - 1].astype(F32)
        return total

    gather_dp(heads, 4)

    def project(j):
        rows = pl.ds(pl.multiple_of(j * 128, 128), 128)
        for s in range(2):
            by_slot = heads[:, :, s * 32 : (s + 1) * 32, :].reshape(512, 512)
            by_request = dot(perm[rows, :], by_slot).astype(BF)
            out = dot(by_request, w_out[...]).astype(BF)
            part[pl.ds(4 * j, 4), s * 32 : (s + 1) * 32, :] = out.reshape(4, 32, 448)

    projected = scatter_tensor(project, part, part_y, part_mid, part_z, 5)
    after[...] = hidden_ref[...].astype(F32) + projected
    x_all[c, t] = after[...].astype(BF)

    for k in (2, 1, 3):
        send(x_all.at[c, t], x_all.at[c, t], 6, k, along_z(k))
    for k in (1, 3, 2):
        arrived(x_all.at[c, y * 4 + lax.rem(zl - k + 4, 4)], 6, k, along_z(-k))

    def quad(core, j):
        return x_all.at[core, pl.ds(4 * j, 4)]

    for k in (2, 1, 3):
        send(quad(c, y), quad(c, y), 6, 4 + k, along_y(k))
    send(quad(c, y), quad(c, y), 6, 8, sibling)

    ones = jnp.ones((8, 448), BF)
    for k in (0, 1, 3, 2):
        j = lax.rem(y - k + 4, 4)
        if k:
            arrived(quad(c, j), 6, 4 + k, along_y(-k))
            send(quad(c, j), quad(c, j), 6, 8 + k, sibling)
        arrived(quad(other, j), 6, 8 + k, sibling)
        rows = [x_all[core, pl.ds(4 * j, 4)].reshape(256, 448) for core in range(2)]
        for n in range(3):
            cols = slice(n * 384, (n + 1) * 384)
            y_part[j, :, cols] = (dot(rows[0], w_mix[0, :, cols]) + dot(rows[1], w_mix[1, :, cols])).astype(BF)
        squares = jnp.zeros((8, 256), F32)
        for core in range(2):
            wide = rows[core].astype(F32)
            square = wide * wide
            high = square.astype(BF)
            squares = squares + dot_nt(ones, high) + dot_nt(ones, (square - high.astype(F32)).astype(BF))
        s_part[j] = squares
        away = lax.rem(j - x + 4, 4)

        @pl.when(away > 0)
        def _():
            remote(y_part.at[j], y_recv.at[away - 1], 7, away, along_x(away)).start()
            remote(s_part.at[j], s_recv.at[away - 1], 8, away, along_x(away)).start()

    for k in (1, 3, 2):
        arrived(y_recv.at[k - 1], 7, k, along_x(-k))
        arrived(s_recv.at[k - 1], 8, k, along_x(-k))
    far_rows = pl.ds(pl.multiple_of((1 - zh) * 128, 128), 128)
    own_rows = pl.ds(pl.multiple_of(zh * 128, 128), 128)

    def x_sum(rows):
        total = y_part[x, rows, :].astype(F32)
        for k in range(3):
            total = total + y_recv[k, rows, :].astype(F32)
        return total

    s_part[x] = s_part[x] + s_recv[0] + s_recv[1] + s_recv[2]
    y_mid[...] = x_sum(far_rows).astype(BF)
    send(y_mid, y_last, 7, 0, z_partner)
    send(s_part.at[x, :, far_rows], s_last, 8, 0, z_partner)
    both = x_sum(own_rows)
    own_squares = s_part[x, :, own_rows]
    arrived(y_last, 7, 0, z_partner)
    arrived(s_last, 8, 0, z_partner)
    both = both + y_last[...].astype(F32)
    inverse = lax.rsqrt((own_squares + s_last[...]) * (1.0 / D) + 1e-6)
    diagonal = iota((128, 128), 0) == iota((128, 128), 1)
    inverse = jnp.sum(jnp.where(diagonal, inverse[0:1, :], 0.0), axis=1, keepdims=True)

    def silu(v):
        return v / (1.0 + jnp.exp(-v))

    both = both * inverse
    acts[c, block, :, 0:512] = (silu(both[:, 0:512]) * both[:, 512:1024]).astype(BF)
    tail = both[:, 1024:1152]
    tail = jnp.where(iota((128, 128), 1) < 64, silu(tail) * pltpu.roll(tail, 64, 1), 0.0)
    acts[c, block, :, 512:640] = jnp.where(c == 0, tail, pltpu.roll(tail, 64, 1)).astype(BF)

    gather_dp(acts, 9)
    load_down.wait()

    def descend(j):
        left = acts[0, pl.ds(2 * j, 2)].reshape(256, 640)
        right = acts[1, pl.ds(2 * j, 2)].reshape(256, 640)
        out = dot(left[:, 0:512], w_down[0:512, :]) + dot(right[:, 0:512], w_down[512:1024, :])
        out = out + dot(left[:, 512:640] + right[:, 512:640], w_down[1024:1152, :])
        down_part[pl.ds(4 * j, 4)] = out.astype(BF).reshape(4, 64, 448)

    fed = scatter_tensor(descend, down_part, down_y, down_mid, down_z, 10)
    o_ref[...] = (x_all[c, t].astype(F32) + fed).astype(BF)

    exchange_end(q_ref, q_recv, 0)
    exchange_end(ql_send, ql_recv, 2)
    exchange_end(ol_send, ol_recv, 3)
    for k in range(1, 4):
        j = lax.rem(x + k, 4)
        remote(y_part.at[j], y_recv.at[k - 1], 7, k, along_x(k)).wait_send()
        remote(s_part.at[j], s_recv.at[k - 1], 8, k, along_x(k)).wait_send()
    for copy in sent:
        copy.wait_send()


def on_device(
    q_nope,
    q_rope,
    cache_latent,
    cache_rope,
    cache_len,
    new_latent,
    new_rope,
    slot_request,
    w_uk,
    w_uv,
    w_out,
    hidden_state,
    norm_gain,
    w_gate,
    w_up,
    w_down,
):
    queries = q_nope.reshape(2, 2, 16, 4, 128).transpose(2, 1, 3, 0, 4).reshape(16, 16, 128)
    rotary = q_rope.transpose(1, 2, 0, 3).reshape(2, 128, 64)
    slots = slot_request.reshape(2, 4, 2, 32).transpose(2, 1, 0, 3).reshape(1, 512)
    gains = jnp.broadcast_to(norm_gain[:, None], (448, 128))
    vmem = pl.BlockSpec(memory_space=pltpu.VMEM)
    anywhere = pl.BlockSpec(memory_space=pl.ANY)

    def buf(*shape, dtype=BF):
        return pltpu.VMEM(shape, dtype)

    out = pl.pallas_call(
        layer_kernel,
        out_shape=jax.ShapeDtypeStruct((64, 448), BF),
        in_specs=[vmem, vmem, pl.BlockSpec(memory_space=pltpu.SMEM), vmem, vmem, vmem, vmem, vmem]
        + [anywhere] * 8,
        out_specs=vmem,
        scratch_shapes=[
            buf(16, 16, 128),
            buf(16, 16, 512),
            buf(16, 16, 512),
            buf(16, 16, 512),
            buf(16, 16, 512),
            buf(2, 2048, 512),
            buf(2, 64, 2048),
            buf(4, 128, 512),
            buf(4, 512, 128),
            buf(512, 448),
            buf(1152, 448),
            buf(2, 448, 1280),
            buf(2, 448, 1152),
            buf(2, 448, 128),
            buf(512, 512),
            buf(2, 8, 64, 512),
            buf(16, 64, 448),
            buf(3, 4, 64, 448),
            buf(4, 64, 448),
            buf(3, 64, 448),
            buf(64, 448, dtype=F32),
            buf(2, 16, 64, 448),
            buf(4, 256, 1152),
            buf(3, 256, 1152),
            buf(4, 8, 256, dtype=F32),
            buf(3, 8, 256, dtype=F32),
            buf(128, 1152),
            buf(128, 1152),
            buf(8, 128, dtype=F32),
            buf(2, 8, 128, 640),
            buf(16, 64, 448),
            buf(3, 4, 64, 448),
            buf(4, 64, 448),
            buf(3, 64, 448),
            pltpu.SemaphoreType.DMA((11,)),
            pltpu.SemaphoreType.DMA((11, 16)),
            pltpu.SemaphoreType.DMA((11, 16)),
        ],
        compiler_params=pltpu.CompilerParams(
            collective_id=0, has_side_effects=True, vmem_limit_bytes=56 * 1024 * 1024
        ),
        name="layer",
    )(
        queries,
        rotary,
        cache_len,
        new_latent,
        new_rope,
        slots,
        gains,
        hidden_state.reshape(64, 448),
        cache_latent,
        cache_rope,
        w_uk,
        w_uv,
        w_out,
        w_gate,
        w_up,
        w_down,
    )
    return out.reshape(2, 32, 448)


def solution(mesh):
    return jax.shard_map(
        on_device,
        mesh=mesh,
        in_specs=(
            P(None, ("dp", "tensor"), None, None),
            P(None, ("dp", "tensor"), None, None),
            P(("dp", "tensor"), None, None),
            P(("dp", "tensor"), None, None),
            P(("dp", "tensor")),
            P(None, ("dp", "tensor"), None),
            P(None, ("dp", "tensor"), None),
            P(),
            P("tensor", None, None),
            P("tensor", None, None),
            P("tensor", "dp"),
            P(None, "tensor", "dp"),
            P("dp"),
            P("dp", "tensor"),
            P("dp", "tensor"),
            P("tensor", "dp"),
        ),
        out_specs=P(None, "tensor", "dp"),
        check_vma=False,
    )
```

```python
import jax
import jax.numpy as jnp
from jax import lax
from jax.experimental import pallas as pl
from jax.experimental.pallas import tpu as pltpu
from jax.sharding import PartitionSpec as P

D = 7168
MESH = pl.DeviceIdType.MESH
BF = jnp.bfloat16
F32 = jnp.float32


def dot(a, b):
    return jnp.dot(a, b, preferred_element_type=F32)


def dot_nt(a, b):
    return lax.dot_general(a, b, (((1,), (1,)), ((), ())), preferred_element_type=F32)


def iota(shape, dim):
    return lax.broadcasted_iota(jnp.int32, shape, dim)


CHUNKS = 4
SPLIT = CHUNKS // 2
RB = 32 // SPLIT


def layer_kernel(
    len_ref,
    new_lat_ref,
    new_rot_ref,
    slot_ref,
    gain_ref,
    hidden_ref,
    q_hbm,
    q_rot_hbm,
    lat_hbm,
    rot_hbm,
    uk_hbm,
    uv_hbm,
    out_hbm,
    gate_hbm,
    up_hbm,
    down_hbm,
    o_ref,
    q_raw,
    q_rot_raw,
    q_send,
    q_recv,
    q_rot,
    ql_send,
    ql_recv,
    ol_send,
    ol_recv,
    lat,
    rot,
    uk,
    uv,
    w_out,
    w_down,
    w_in,
    w_mix,
    gains,
    perm,
    heads,
    part,
    part_y,
    part_mid,
    part_z,
    x_all,
    y_part,
    y_recv,
    s_part,
    s_recv,
    y_mid,
    y_last,
    s_mid,
    s_last,
    acts,
    down_part,
    down_y,
    down_mid,
    down_z,
    local_sem,
    send_sem,
    recv_sem,
):
    d = lax.axis_index("dp")
    t = lax.axis_index("tensor")
    zh = lax.div(d, 8)
    x = lax.rem(lax.div(d, 2), 4)
    c = lax.rem(d, 2)
    y = lax.div(t, 4)
    zl = lax.rem(t, 4)
    other = 1 - c
    sibling = (d + 1 - 2 * c, t)
    z_partner = (lax.rem(d + 8, 16), t)
    block = x * 2 + zh
    far = x * 2 + 1 - zh

    def along_x(k):
        return (zh * 8 + lax.rem(x + k + 4, 4) * 2 + c, t)

    def along_y(k):
        return (d, lax.rem(y + k + 4, 4) * 4 + zl)

    def along_z(k):
        return (d, y * 4 + lax.rem(zl + k + 4, 4))

    sent = []
    phases = {}

    def remote(src, dst, phase, i, device):
        n = phases.setdefault(phase, len(phases))
        return pltpu.make_async_remote_copy(
            src_ref=src,
            dst_ref=dst,
            send_sem=send_sem.at[n, i],
            recv_sem=recv_sem.at[n, i],
            device_id=device,
            device_id_type=MESH,
        )

    def send(src, dst, phase, i, device):
        copy = remote(src, dst, phase, i, device)
        copy.start()
        sent.append(copy)

    def arrived(dst, phase, i, device):
        remote(dst, dst, phase, i, device).wait_recv()

    def all_sent():
        for copy in sent:
            copy.wait_send()
        sent.clear()

    def load(src, dst, i):
        copy = pltpu.make_async_copy(src, dst, local_sem.at[i])
        copy.start()
        return copy

    load_q = load(q_hbm, q_raw, 0)
    load_uk = load(uk_hbm, uk, 1)
    load_q_rot = load(q_rot_hbm, q_rot_raw, 2)
    mine = pl.ds(pl.multiple_of(c * 512, 512), 512)
    load_in = [
        load(gate_hbm.at[:, mine], w_in.at[c, :, pl.ds(0, 512)], 3),
        load(up_hbm.at[:, mine], w_in.at[c, :, pl.ds(512, 512)], 4),
        load(gate_hbm.at[:, pl.ds(1024, 128)], w_in.at[c, :, pl.ds(1024, 128)], 5),
        load(up_hbm.at[:, pl.ds(1024, 128)], w_in.at[c, :, pl.ds(1152, 128)], 6),
    ]
    load_lat = load(lat_hbm, lat, 7)
    load_rot = load(rot_hbm, rot, 8)
    load_uv = load(uv_hbm, uv, 9)
    load_out = load(out_hbm, w_out, 10)
    load_down = load(down_hbm, w_down, 11)

    barrier = pltpu.get_barrier_semaphore()
    for device in (z_partner, along_x(2), along_x(1), along_x(3), sibling):
        pl.semaphore_signal(barrier, inc=1, device_id=device, device_id_type=MESH)

    def greet(i, carry):
        pl.semaphore_signal(
            barrier, inc=1, device_id=(d, lax.rem(t + i, 16)), device_id_type=MESH
        )
        return carry

    lax.fori_loop(1, 16, greet, 0)

    row = iota((256, 256), 0)
    col = iota((256, 256), 1)
    source = (
        lax.rem(row, 2) * 128
        + lax.div(lax.rem(row, 16), 8) * 64
        + lax.div(row, 16) * 4
        + lax.div(lax.rem(row, 8), 2)
    )
    by_block = jnp.where(col == source, 1.0, 0.0).astype(BF)
    load_q.wait()
    q_send[...] = dot(by_block, q_raw[...].reshape(256, 128)).astype(BF).reshape(16, 16, 128)
    gains[c] = jnp.broadcast_to(gain_ref[...].astype(F32), (8, 448))
    pl.semaphore_wait(barrier, 20)

    def exchange_start(src, dst, phase):
        def one(i, carry):
            p = lax.rem(t + i, 16)
            remote(src.at[p], dst.at[t], phase, i, (d, p)).start()
            return carry

        lax.fori_loop(1, 16, one, 0)
        dst[t] = src[t]

    def exchange_wait(src, dst, phase):
        def one(i, carry):
            p = lax.rem(t + 16 - i, 16)
            remote(src.at[p], dst.at[p], phase, i, (d, p)).wait_recv()
            return carry

        lax.fori_loop(1, 16, one, 0)

    def exchange_end(src, dst, phase):
        def one(i, carry):
            p = lax.rem(t + i, 16)
            remote(src.at[p], dst.at[t], phase, i, (d, p)).wait_send()
            return carry

        lax.fori_loop(1, 16, one, 0)

    exchange_start(q_send, q_recv, "q")

    theirs = pl.ds(pl.multiple_of(other * 512, 512), 512)
    send(gains.at[c], gains.at[c], "w", 4, sibling)
    send(gate_hbm.at[:, theirs], w_in.at[c, :, pl.ds(0, 512)], "w", 0, sibling)
    send(up_hbm.at[:, theirs], w_in.at[c, :, pl.ds(512, 512)], "w", 1, sibling)
    send(gate_hbm.at[:, pl.ds(1024, 128)], w_in.at[c, :, pl.ds(1024, 128)], "w", 2, sibling)
    send(up_hbm.at[:, pl.ds(1024, 128)], w_in.at[c, :, pl.ds(1152, 128)], "w", 3, sibling)

    head_of_row = lax.div(lax.rem(iota((256, 512), 0), 8), 2)
    source = lax.rem(row, 2) * 128 + lax.div(row, 128) * 64 + lax.div(lax.rem(row, 128), 2)
    by_slot = jnp.where(col == source, 1.0, 0.0).astype(BF)
    load_q_rot.wait()
    q_rot[...] = dot(by_slot, q_rot_raw[...].reshape(256, 64)).astype(BF).reshape(2, 128, 64)
    load_uk.wait()
    exchange_wait(q_send, q_recv, "q")
    q_rows = q_recv[...].reshape(256, 128)
    q_lat = jnp.zeros((256, 512), F32)
    for j in range(4):
        q_lat = jnp.where(head_of_row == j, dot(q_rows, uk[j]), q_lat)
    ql_send[...] = q_lat.astype(BF).reshape(16, 16, 512)
    exchange_start(ql_send, ql_recv, "ql")

    row = iota((512, 512), 0)
    span = 512 // SPLIT
    request = (
        lax.div(lax.rem(row, span), RB) * 32 + lax.div(row, span) * RB + lax.rem(row, RB)
    )
    perm[...] = jnp.where(request == slot_ref[...], 1.0, 0.0).astype(BF)
    for copy in load_in:
        copy.wait()
    arrived(w_in.at[other, :, pl.ds(0, 512)], "w", 0, sibling)
    arrived(w_in.at[other, :, pl.ds(512, 512)], "w", 1, sibling)
    arrived(w_in.at[other, :, pl.ds(1024, 128)], "w", 2, sibling)
    arrived(w_in.at[other, :, pl.ds(1152, 128)], "w", 3, sibling)
    arrived(gains.at[other], "w", 4, sibling)
    low = iota((448, 128), 1) < 64
    eye = iota((448, 448), 0) == iota((448, 448), 1)
    for k in range(2):
        gain = jnp.sum(jnp.where(eye, gains[k, 0:1, :], 0.0), axis=1, keepdims=True)
        for j in range(8):
            cols = pl.ds(j * 128, 128)
            w_mix[k, :, cols] = (w_in[k, :, cols].astype(F32) * gain).astype(BF)
        gate_tail = w_in[k, :, pl.ds(1024, 128)].astype(F32)
        up_tail = w_in[k, :, pl.ds(1152, 128)].astype(F32)
        first = jnp.where(low, gate_tail, pltpu.roll(up_tail, 64, 1))
        second = jnp.where(low, pltpu.roll(gate_tail, 64, 1), up_tail)
        tail = jnp.where(c == 0, first, second)
        w_mix[k, :, pl.ds(1024, 128)] = (tail * gain).astype(BF)

    load_lat.wait()
    load_rot.wait()
    exchange_wait(ql_send, ql_recv, "ql")
    scale = 1.0 / 192.0**0.5
    step = lax.rem(iota((128, 1), 0), 2)
    q_all = ql_recv[...].astype(F32)
    results = []
    for r in range(2):
        q_wide = q_all[:, 8 * r : 8 * r + 8, :].reshape(128, 512)
        q = q_wide.astype(BF)
        q_turned = q_rot[r]
        scores = (dot_nt(q, lat[r]) + dot(q_turned, rot[r])) * scale
        scores = jnp.where(iota((128, 2048), 1) < len_ref[r], scores, -1e30)
        q_turned_wide = q_turned.astype(F32)
        top = jnp.max(scores, axis=1, keepdims=True)
        fresh = []
        for u in range(2):
            value = jnp.sum(q_wide * new_lat_ref[u, r : r + 1, :].astype(F32), axis=1, keepdims=True)
            value = value + jnp.sum(
                q_turned_wide * new_rot_ref[u, r : r + 1, :].astype(F32), axis=1, keepdims=True
            )
            value = jnp.where(step >= u, value * scale, -1e30)
            top = jnp.maximum(top, value)
            fresh.append(value)
        weights = jnp.exp(scores - top)
        total = jnp.sum(weights, axis=1, keepdims=True)
        mixed = dot(weights.astype(BF), lat[r])
        for u in range(2):
            weight = jnp.exp(fresh[u] - top)
            total = total + weight
            mixed = mixed + weight * new_lat_ref[u, r : r + 1, :].astype(F32)
        results.append((mixed / total).reshape(16, 8, 512))
    ol_send[...] = jnp.concatenate(results, axis=1).astype(BF)

    exchange_start(ol_send, ol_recv, "ol")
    load_uv.wait()
    load_out.wait()
    load_down.wait()
    exchange_end(q_send, q_recv, "q")
    exchange_end(ql_send, ql_recv, "ql")
    row = iota((64, 256), 0)
    col = iota((64, 256), 1)
    pick = (
        (lax.div(row, 32) == lax.rem(col, 2))
        & (lax.div(lax.rem(row, 32), 2) == lax.div(col, 16))
        & (lax.rem(row, 2) == lax.rem(lax.div(col, 8), 2))
    )
    pick = jnp.where(pick, 1.0, 0.0).astype(BF)
    own_head = lax.div(lax.rem(iota((256, 128), 0), 8), 2)
    exchange_wait(ol_send, ol_recv, "ol")
    o_rows = ol_recv[...].reshape(256, 512)
    spread = [jnp.where(own_head == j, dot(o_rows, uv[j]), 0.0).astype(BF) for j in range(4)]
    head_rows = dot(pick, jnp.concatenate(spread, axis=1)).astype(BF)
    for s in range(2):
        heads[s, c, block] = head_rows[32 * s : 32 * s + 32]

    def gather_1(buf, phase):
        send(buf.at[c, block], buf.at[c, block], phase, 0, z_partner)

    def pair(buf, core, j):
        return buf.at[core, pl.ds(2 * j, 2)]

    def gather_2(buf, phase):
        arrived(buf.at[c, far], phase, 0, z_partner)
        for k in (2, 1, 3):
            send(pair(buf, c, x), pair(buf, c, x), phase, k, along_x(k))
        send(pair(buf, c, x), pair(buf, c, x), phase, 4, sibling)

    def gather_3(buf, phase):
        for k in (1, 3, 2):
            j = lax.rem(x - k + 4, 4)
            arrived(pair(buf, c, j), phase, k, along_x(-k))
            send(pair(buf, c, j), pair(buf, c, j), phase, 4 + k, sibling)

    def gather_4(buf, phase):
        for k in range(4):
            j = lax.rem(x - k + 4, 4)
            arrived(pair(buf, other, j), phase, 4 + k, sibling)

    def scatter_1(buf, from_y, phase):
        for k in (2, 1, 3):
            j = lax.rem(y + k, 4)
            send(buf.at[pl.ds(4 * j, 4)], from_y.at[k - 1], phase, k, along_y(k))

    def scatter_2(buf, from_y, mid, from_z, phase):
        total = buf[pl.ds(4 * y, 4)].astype(F32)
        for k in (1, 3, 2):
            arrived(from_y.at[k - 1], phase, k, along_y(-k))
            total = total + from_y[k - 1].astype(F32)
        mid[...] = total.astype(BF)
        for k in (2, 1, 3):
            send(mid.at[lax.rem(zl + k, 4)], from_z.at[k - 1], phase, 4 + k, along_z(k))

    def scatter_3(mid, from_z, phase):
        total = mid[zl].astype(F32)
        for k in (1, 3, 2):
            arrived(from_z.at[k - 1], phase, 4 + k, along_z(-k))
            total = total + from_z[k - 1].astype(F32)
        return total

    def quad(g, core, j):
        return x_all.at[g, core, pl.ds(4 * j, 4)]

    def silu(v):
        return v / (1.0 + jnp.exp(-v))

    ones = jnp.ones((8, 448), BF)
    far_rows = pl.ds(pl.multiple_of((1 - zh) * 2 * RB, 2 * RB), 2 * RB)
    own_rows = pl.ds(pl.multiple_of(zh * 2 * RB, 2 * RB), 2 * RB)

    def out_rows(g):
        start = (g // SPLIT) * 32 + (g % SPLIT) * RB
        return slice(start, start + RB)

    def project(g):
        s, half = g // SPLIT, g % SPLIT
        if half == 0:
            gather_4(heads.at[s], ("heads", s))
        ordered = jnp.concatenate(
            [heads[s, n % 2, (n // 2 % 4) * 2 + n // 8] for n in range(16)], axis=0
        )
        by_request = dot(perm[half * span : (half + 1) * span, :], ordered).astype(BF)
        part[g] = dot_nt(by_request, w_out[...]).astype(BF).reshape(16, RB, 448)
        scatter_1(part.at[g], part_y.at[g], ("out", g))

    def project_2(g):
        scatter_2(part.at[g], part_y.at[g], part_mid.at[g], part_z.at[g], ("out", g))

    def residual(g):
        total = scatter_3(part_mid.at[g], part_z.at[g], ("out", g))
        x_all[g, c, t] = (hidden_ref[out_rows(g), :].astype(F32) + total).astype(BF)
        for k in (2, 1, 3):
            send(x_all.at[g, c, t], x_all.at[g, c, t], ("x", g), k, along_z(k))

    def spread_y(g):
        for k in (1, 3, 2):
            arrived(x_all.at[g, c, y * 4 + lax.rem(zl - k + 4, 4)], ("x", g), k, along_z(-k))
        for k in (2, 1, 3):
            send(quad(g, c, y), quad(g, c, y), ("x", g), 4 + k, along_y(k))
        send(quad(g, c, y), quad(g, c, y), ("x", g), 8, sibling)

    def spread_core(g):
        for k in (1, 3, 2):
            j = lax.rem(y - k + 4, 4)
            arrived(quad(g, c, j), ("x", g), 4 + k, along_y(-k))
            send(quad(g, c, j), quad(g, c, j), ("x", g), 8 + k, sibling)

    def gate_up(g):
        for k in range(4):
            arrived(quad(g, other, lax.rem(y - k + 4, 4)), ("x", g), 8 + k, sibling)
        rows = [x_all[g, core].reshape(16 * RB, 448) for core in range(2)]
        for n in range(3):
            cols = slice(n * 384, (n + 1) * 384)
            value = dot(rows[0], w_mix[0, :, cols]) + dot(rows[1], w_mix[1, :, cols])
            y_part[g, :, :, cols] = value.astype(BF).reshape(4, 4 * RB, 384)
        squares = jnp.zeros((8, 16 * RB), F32)
        for core in range(2):
            wide = rows[core].astype(F32)
            square = wide * wide
            high = square.astype(BF)
            squares = squares + dot_nt(ones, high) + dot_nt(ones, (square - high.astype(F32)).astype(BF))
        for n in range(8):
            s_part[g, n // 2, n % 2, :, 0 : 2 * RB] = squares[:, n * 2 * RB : (n + 1) * 2 * RB]
        for k in (2, 1, 3):
            j = lax.rem(x + k, 4)
            send(y_part.at[g, j], y_recv.at[g, k - 1], ("gate", g), k, along_x(k))
            send(s_part.at[g, j], s_recv.at[g, k - 1], ("gate", g), 4 + k, along_x(k))

    def x_sum(g, rows):
        total = y_part[g, x, rows, :].astype(F32)
        for k in range(3):
            total = total + y_recv[g, k, rows, :].astype(F32)
        return total

    def s_sum(g, half):
        total = s_part[g, x, half]
        for k in range(3):
            total = total + s_recv[g, k, half]
        return total

    def gate_z(g):
        for k in (1, 3, 2):
            arrived(y_recv.at[g, k - 1], ("gate", g), k, along_x(-k))
            arrived(s_recv.at[g, k - 1], ("gate", g), 4 + k, along_x(-k))
        y_mid[g] = x_sum(g, far_rows).astype(BF)
        s_mid[g] = s_sum(g, 1 - zh)
        send(y_mid.at[g], y_last.at[g], ("gate", g), 0, z_partner)
        send(s_mid.at[g], s_last.at[g], ("gate", g), 4, z_partner)

    def activate(g):
        both = x_sum(g, own_rows)
        squares = s_sum(g, zh)
        arrived(y_last.at[g], ("gate", g), 0, z_partner)
        arrived(s_last.at[g], ("gate", g), 4, z_partner)
        squares = (squares + s_last[g])[0:1, 0 : 2 * RB]
        inverse = lax.rsqrt(squares * (1.0 / D) + 1e-6)
        diagonal = iota((2 * RB, 2 * RB), 0) == iota((2 * RB, 2 * RB), 1)
        inverse = jnp.sum(jnp.where(diagonal, inverse, 0.0), axis=1, keepdims=True)
        both = (both + y_last[g].astype(F32)) * inverse
        acts[g, c, block, :, 0:512] = (silu(both[:, 0:512]) * both[:, 512:1024]).astype(BF)
        tail = both[:, 1024:1152]
        tail = jnp.where(
            iota((2 * RB, 128), 1) < 64, silu(tail) * pltpu.roll(tail, 64, 1), 0.0
        )
        acts[g, c, block, :, 512:640] = jnp.where(c == 0, tail, pltpu.roll(tail, 64, 1)).astype(BF)
        gather_1(acts.at[g], ("act", g))

    def act_x(g):
        gather_2(acts.at[g], ("act", g))

    def act_core(g):
        gather_3(acts.at[g], ("act", g))

    def descend(g):
        gather_4(acts.at[g], ("act", g))
        left = acts[g, 0].reshape(16 * RB, 640)
        right = acts[g, 1].reshape(16 * RB, 640)
        out = dot_nt(left[:, 0:512], w_down[:, 0:512]) + dot_nt(right[:, 0:512], w_down[:, 512:1024])
        out = out + dot_nt(left[:, 512:640] + right[:, 512:640], w_down[:, 1024:1152])
        down_part[g] = out.astype(BF).reshape(16, RB, 448)
        scatter_1(down_part.at[g], down_y.at[g], ("down", g))

    def descend_2(g):
        scatter_2(down_part.at[g], down_y.at[g], down_mid.at[g], down_z.at[g], ("down", g))

    def finish(g):
        if g == CHUNKS - 1:
            all_sent()
            exchange_end(ol_send, ol_recv, "ol")
        fed = scatter_3(down_mid.at[g], down_z.at[g], ("down", g))
        o_ref[out_rows(g), :] = (x_all[g, c, t].astype(F32) + fed).astype(BF)

    for s in range(2):
        gather_1(heads.at[s], ("heads", s))
    for s in range(2):
        gather_2(heads.at[s], ("heads", s))
    stages = [
        project,
        project_2,
        residual,
        spread_y,
        spread_core,
        gate_up,
        gate_z,
        activate,
        act_x,
        act_core,
        descend,
        descend_2,
        finish,
    ]
    for tick in range(len(stages) + CHUNKS - 1):
        if tick in (0, SPLIT):
            gather_3(heads.at[tick // SPLIT], ("heads", tick // SPLIT))
        for g in range(CHUNKS):
            if 0 <= tick - g < len(stages):
                stages[tick - g](g)
    all_sent()


def on_device(
    q_nope,
    q_rope,
    cache_latent,
    cache_rope,
    cache_len,
    new_latent,
    new_rope,
    slot_request,
    w_uk,
    w_uv,
    w_out,
    hidden_state,
    norm_gain,
    w_gate,
    w_up,
    w_down,
):
    vmem = pl.BlockSpec(memory_space=pltpu.VMEM)
    anywhere = pl.BlockSpec(memory_space=pl.ANY)

    def buf(*shape, dtype=BF):
        return pltpu.VMEM(shape, dtype)

    out = pl.pallas_call(
        layer_kernel,
        out_shape=jax.ShapeDtypeStruct((64, 448), BF),
        in_specs=[pl.BlockSpec(memory_space=pltpu.SMEM), vmem, vmem, vmem, vmem, vmem]
        + [anywhere] * 10,
        out_specs=vmem,
        scratch_shapes=[
            buf(2, 2, 64, 128),
            buf(2, 2, 64, 64),
            buf(16, 16, 128),
            buf(16, 16, 128),
            buf(2, 128, 64),
            buf(16, 16, 512),
            buf(16, 16, 512),
            buf(16, 16, 512),
            buf(16, 16, 512),
            buf(2, 2048, 512),
            buf(2, 64, 2048),
            buf(4, 128, 512),
            buf(4, 512, 128),
            buf(448, 512),
            buf(448, 1152),
            buf(2, 448, 1280),
            buf(2, 448, 1152),
            buf(2, 8, 448, dtype=F32),
            buf(512, 512),
            buf(2, 2, 8, 32, 512),
            buf(CHUNKS, 16, RB, 448),
            buf(CHUNKS, 3, 4, RB, 448),
            buf(CHUNKS, 4, RB, 448),
            buf(CHUNKS, 3, RB, 448),
            buf(CHUNKS, 2, 16, RB, 448),
            buf(CHUNKS, 4, 4 * RB, 1152),
            buf(CHUNKS, 3, 4 * RB, 1152),
            buf(CHUNKS, 4, 2, 8, 128, dtype=F32),
            buf(CHUNKS, 3, 2, 8, 128, dtype=F32),
            buf(CHUNKS, 2 * RB, 1152),
            buf(CHUNKS, 2 * RB, 1152),
            buf(CHUNKS, 8, 128, dtype=F32),
            buf(CHUNKS, 8, 128, dtype=F32),
            buf(CHUNKS, 2, 8, 2 * RB, 640),
            buf(CHUNKS, 16, RB, 448),
            buf(CHUNKS, 3, 4, RB, 448),
            buf(CHUNKS, 4, RB, 448),
            buf(CHUNKS, 3, RB, 448),
            pltpu.SemaphoreType.DMA((12,)),
            pltpu.SemaphoreType.DMA((6 + 5 * CHUNKS, 16)),
            pltpu.SemaphoreType.DMA((6 + 5 * CHUNKS, 16)),
        ],
        compiler_params=pltpu.CompilerParams(
            collective_id=0, has_side_effects=True, vmem_limit_bytes=56 * 1024 * 1024
        ),
        name="layer",
    )(
        cache_len,
        new_latent,
        new_rope,
        slot_request.reshape(1, 512),
        norm_gain.reshape(1, 448),
        hidden_state.reshape(64, 448),
        q_nope,
        q_rope,
        cache_latent,
        cache_rope,
        w_uk,
        w_uv,
        w_out.T,
        w_gate,
        w_up,
        w_down.T,
    )
    return out.reshape(2, 32, 448)


def solution(mesh):
    return jax.shard_map(
        on_device,
        mesh=mesh,
        in_specs=(
            P(None, ("dp", "tensor"), None, None),
            P(None, ("dp", "tensor"), None, None),
            P(("dp", "tensor"), None, None),
            P(("dp", "tensor"), None, None),
            P(("dp", "tensor")),
            P(None, ("dp", "tensor"), None),
            P(None, ("dp", "tensor"), None),
            P(),
            P("tensor", None, None),
            P("tensor", None, None),
            P("tensor", "dp"),
            P(None, "tensor", "dp"),
            P("dp"),
            P("dp", "tensor"),
            P("dp", "tensor"),
            P("tensor", "dp"),
        ),
        out_specs=P(None, "tensor", "dp"),
        check_vma=False,
    )
```

```python
import jax
import jax.numpy as jnp
from jax import lax
from jax.experimental import pallas as pl
from jax.experimental.pallas import tpu as pltpu
from jax.sharding import PartitionSpec as P

D = 7168
MESH = pl.DeviceIdType.MESH
BF = jnp.bfloat16
F32 = jnp.float32


def dot(a, b):
    return jnp.dot(a, b, preferred_element_type=F32)


def dot_nt(a, b):
    return lax.dot_general(a, b, (((1,), (1,)), ((), ())), preferred_element_type=F32)


def iota(shape, dim):
    return lax.broadcasted_iota(jnp.int32, shape, dim)


CHUNKS = 4
SPLIT = CHUNKS // 2
RB = 32 // SPLIT
ORDER = "01010ab1adcabdabdabacdbbcddcacbcadbacdbaacbdbacadbdccbdcdc"


def layer_kernel(
    len_ref,
    slot_ref,
    gain_ref,
    new_lat_hbm,
    new_rot_hbm,
    hidden_hbm,
    q_hbm,
    q_rot_hbm,
    lat_hbm,
    rot_hbm,
    uk_hbm,
    uv_hbm,
    out_hbm,
    gate_hbm,
    up_hbm,
    down_hbm,
    o_ref,
    new_lat_ref,
    new_rot_ref,
    hidden_ref,
    q_raw,
    q_rot_raw,
    q_send,
    q_recv,
    ql_send,
    ql_recv,
    ol_send,
    ol_recv,
    lat,
    rot,
    uk,
    uv,
    w_out,
    w_down,
    w_in,
    w_mix,
    gains,
    perm,
    by_block,
    picks,
    to_slots,
    to_blocks,
    pick,
    heads,
    part,
    part_y,
    part_mid,
    part_z,
    x_all,
    y_part,
    y_recv,
    s_part,
    s_recv,
    y_mid,
    y_last,
    s_mid,
    s_last,
    acts,
    down_part,
    down_y,
    down_mid,
    down_z,
    local_sem,
    send_sem,
    recv_sem,
):
    d = lax.axis_index("dp")
    t = lax.axis_index("tensor")
    zh = lax.div(d, 8)
    x = lax.rem(lax.div(d, 2), 4)
    c = lax.rem(d, 2)
    y = lax.div(t, 4)
    zl = lax.rem(t, 4)
    other = 1 - c
    sibling = (d + 1 - 2 * c, t)
    z_partner = (lax.rem(d + 8, 16), t)
    block = x * 2 + zh
    far = x * 2 + 1 - zh

    def along_x(k):
        return (zh * 8 + lax.rem(x + k + 4, 4) * 2 + c, t)

    def along_y(k):
        return (d, lax.rem(y + k + 4, 4) * 4 + zl)

    def along_z(k):
        return (d, y * 4 + lax.rem(zl + k + 4, 4))

    sent = []
    groups = {}

    def remote(src, dst, group, device):
        n = groups.setdefault(group, len(groups))
        return pltpu.make_async_remote_copy(
            src_ref=src,
            dst_ref=dst,
            send_sem=send_sem.at[n],
            recv_sem=recv_sem.at[n],
            device_id=device,
            device_id_type=MESH,
        )

    def send(src, dst, group, device):
        remote(src, dst, group, device).start()

    def arrived(whole, group):
        remote(whole, whole, group, sibling).wait_recv()
        sent.append(remote(whole, whole, group, sibling))

    def all_sent():
        for copy in sent:
            copy.wait_send()
        sent.clear()

    def one_hot(ref, mask):
        ref[...] = jnp.where(mask, 1.0, 0.0).astype(BF)

    def load(src, dst, i):
        copy = pltpu.make_async_copy(src, dst, local_sem.at[i])
        copy.start()
        return copy

    load_q = load(q_hbm, q_raw, 0)
    load_uk = load(uk_hbm, uk, 1)
    load_q_rot = load(q_rot_hbm, q_rot_raw, 2)
    mine = pl.ds(pl.multiple_of(c * 512, 512), 512)
    load_in = [
        load(gate_hbm.at[:, mine], w_in.at[c, :, pl.ds(0, 512)], 3),
        load(up_hbm.at[:, mine], w_in.at[c, :, pl.ds(512, 512)], 4),
        load(gate_hbm.at[:, pl.ds(1024, 128)], w_in.at[c, :, pl.ds(1024, 128)], 5),
        load(up_hbm.at[:, pl.ds(1024, 128)], w_in.at[c, :, pl.ds(1152, 128)], 6),
    ]
    load_small = [
        load(new_lat_hbm, new_lat_ref, 12),
        load(new_rot_hbm, new_rot_ref, 13),
        load(hidden_hbm, hidden_ref, 14),
    ]
    load_lat = load(lat_hbm, lat, 7)
    load_rot = load(rot_hbm, rot, 8)
    load_uv = load(uv_hbm, uv, 9)
    load_out = load(out_hbm, w_out, 10)
    load_down = load(down_hbm, w_down, 11)

    barrier = pltpu.get_barrier_semaphore()
    for device in (z_partner, along_x(2), along_x(1), along_x(3), sibling):
        pl.semaphore_signal(barrier, inc=1, device_id=device, device_id_type=MESH)

    def greet(i, carry):
        pl.semaphore_signal(
            barrier, inc=1, device_id=(d, lax.rem(t + i, 16)), device_id_type=MESH
        )
        return carry

    lax.fori_loop(1, 16, greet, 0)

    row = iota((256, 256), 0)
    col = iota((256, 256), 1)
    source = ((row & 8) << 4) + ((row & 4) << 4) + ((row >> 4) << 2) + (row & 3)
    one_hot(by_block, col == source)
    for s in range(2):
        one_hot(picks.at[s], col == ((row >> 4) << 4) + 8 * s + (row & 7))
    def position(m, half):
        return ((m & 60) << 2) + half * 8 + ((m >> 6) << 2) + (m & 3)

    for half in range(2):
        one_hot(to_slots.at[half], iota((128, 256), 1) == position(iota((128, 256), 0), half))
        one_hot(to_blocks.at[half], iota((256, 128), 0) == position(iota((256, 128), 1), half))
    col = iota((32, 128), 1)
    one_hot(pick, (((col & 60) >> 1) + (col >> 6)) == iota((32, 128), 0))
    row = iota((512, 512), 0)
    span = 512 // SPLIT
    if SPLIT == 1:
        request = row
    else:
        request = ((row & 255) >> 4 << 5) + (row >> 8 << 4) + (row & 15)
    one_hot(perm, request == slot_ref[...])
    load_q.wait()
    q_send[...] = dot(by_block[...], q_raw[...].reshape(256, 128)).astype(BF).reshape(16, 16, 128)
    gains[c] = jnp.broadcast_to(gain_ref[...].astype(F32).reshape(1, 448), (8, 448))
    pl.semaphore_wait(barrier, 20)

    def exchange_start(src, dst, group):
        def one(i, carry):
            p = lax.rem(t + i, 16)
            send(src.at[p], dst.at[t], group, (d, p))
            return carry

        lax.fori_loop(1, 16, one, 0)
        dst[t] = src[t]

    def exchange_wait(dst, group):
        arrived(dst.at[pl.ds(0, 15)], group)

    exchange_start(q_send, q_recv, "q")

    theirs = pl.ds(pl.multiple_of(other * 512, 512), 512)
    send(gains.at[c], gains.at[c], ("w", 4), sibling)
    send(gate_hbm.at[:, theirs], w_in.at[c, :, pl.ds(0, 512)], ("w", 0), sibling)
    send(up_hbm.at[:, theirs], w_in.at[c, :, pl.ds(512, 512)], ("w", 1), sibling)
    send(gate_hbm.at[:, pl.ds(1024, 128)], w_in.at[c, :, pl.ds(1024, 128)], ("w", 2), sibling)
    send(up_hbm.at[:, pl.ds(1024, 128)], w_in.at[c, :, pl.ds(1152, 128)], ("w", 3), sibling)

    head_of_row = iota((256, 512), 0) & 3
    first_half = (iota((256, 256), 0) & 8) == 0
    load_uk.wait()
    exchange_wait(q_recv, "q")
    q_all = q_recv[...].reshape(256, 128)
    for s in range(2):
        q_rows = dot(picks[s], q_all).astype(BF)
        q_lat = jnp.zeros((256, 512), F32)
        for j in range(4):
            q_lat = jnp.where(head_of_row == j, dot(q_rows, uk[j]), q_lat)
        q_lat = jnp.where(first_half, q_lat[:, 0:256], q_lat[:, 256:512])
        ql_send[s] = q_lat.astype(BF).reshape(16, 16, 256)
        exchange_start(ql_send.at[s], ql_recv.at[s], ("ql", s))

    def slot_rows(blocks):
        blocks = blocks.reshape(256, 256)
        return jnp.concatenate([dot(to_slots[0], blocks), dot(to_slots[1], blocks)], axis=1)

    load_q_rot.wait()
    for copy in load_small:
        copy.wait()
    load_lat.wait()
    load_rot.wait()
    scale = 1.0 / 192.0**0.5
    for s in range(2):
        exchange_wait(ql_recv.at[s], ("ql", s))
        q_rows = slot_rows(ql_recv[s])
        results = []
        for r in range(2):
            q_wide = q_rows[64 * r : 64 * r + 64, :]
            q_turned = q_rot_raw[s, r]
            scores = (dot_nt(q_wide.astype(BF), lat[r]) + dot(q_turned, rot[r])) * scale
            scores = jnp.where(iota((64, 2048), 1) < len_ref[r], scores, -1e30)
            q_turned_wide = q_turned.astype(F32)
            top = jnp.max(scores, axis=1, keepdims=True)
            fresh = []
            for u in range(s + 1):
                value = jnp.sum(
                    q_wide * new_lat_ref[u, r : r + 1, :].astype(F32), axis=1, keepdims=True
                )
                value = value + jnp.sum(
                    q_turned_wide * new_rot_ref[u, r : r + 1, :].astype(F32), axis=1, keepdims=True
                )
                value = value * scale
                top = jnp.maximum(top, value)
                fresh.append(value)
            weights = jnp.exp(scores - top)
            total = jnp.sum(weights, axis=1, keepdims=True)
            mixed = dot(weights.astype(BF), lat[r])
            for u in range(s + 1):
                weight = jnp.exp(fresh[u] - top)
                total = total + weight
                mixed = mixed + weight * new_lat_ref[u, r : r + 1, :].astype(F32)
            results.append((mixed / total).astype(BF))
        mixed = jnp.concatenate(results, axis=0)
        mixed = dot(to_blocks[0], mixed[:, 0:256]) + dot(to_blocks[1], mixed[:, 256:512])
        ol_send[s] = mixed.astype(BF).reshape(16, 16, 256)
        exchange_start(ol_send.at[s], ol_recv.at[s], ("ol", s))

    for copy in load_in:
        copy.wait()
    arrived(w_in.at[other, :, pl.ds(0, 512)], ("w", 0))
    arrived(w_in.at[other, :, pl.ds(512, 512)], ("w", 1))
    arrived(w_in.at[other, :, pl.ds(1024, 128)], ("w", 2))
    arrived(w_in.at[other, :, pl.ds(1152, 128)], ("w", 3))
    arrived(gains.at[other], ("w", 4))
    low = iota((448, 128), 1) < 64
    eye = iota((448, 448), 0) == iota((448, 448), 1)
    for k in range(2):
        gain = jnp.sum(jnp.where(eye, gains[k, 0:1, :], 0.0), axis=1, keepdims=True)
        for j in range(8):
            cols = pl.ds(j * 128, 128)
            w_mix[k, :, cols] = (w_in[k, :, cols].astype(F32) * gain).astype(BF)
        gate_tail = w_in[k, :, pl.ds(1024, 128)].astype(F32)
        up_tail = w_in[k, :, pl.ds(1152, 128)].astype(F32)
        first = jnp.where(low, gate_tail, pltpu.roll(up_tail, 64, 1))
        second = jnp.where(low, pltpu.roll(gate_tail, 64, 1), up_tail)
        tail = jnp.where(c == 0, first, second)
        w_mix[k, :, pl.ds(1024, 128)] = (tail * gain).astype(BF)

    load_uv.wait()
    load_out.wait()
    load_down.wait()
    own_head = iota((128, 128), 0) & 3

    def head_outputs(s):
        exchange_wait(ol_recv.at[s], ("ol", s))
        o_rows = slot_rows(ol_recv[s]).astype(BF)
        spread = [jnp.where(own_head == j, dot(o_rows, uv[j]), 0.0).astype(BF) for j in range(4)]
        heads[s, c, block] = dot(pick[...], jnp.concatenate(spread, axis=1)).astype(BF)
        gather_1(heads.at[s], ("heads", s))

    def gather_1(buf, group):
        send(buf.at[c, block], buf.at[c, block], group + ("z",), z_partner)

    def pair(buf, j):
        return buf.at[c, pl.ds(2 * j, 2)]

    def gather_2(buf, group):
        arrived(buf.at[c, far], group + ("z",))
        for k in (2, 1, 3):
            send(pair(buf, x), pair(buf, x), group + ("x",), along_x(k))
        send(pair(buf, x), pair(buf, x), group + ("core",), sibling)

    def gather_3(buf, group):
        arrived(buf.at[c, pl.ds(0, 6)], group + ("x",))
        for k in range(1, 4):
            j = lax.rem(x + k, 4)
            send(pair(buf, j), pair(buf, j), group + ("core",), sibling)

    def gather_4(buf, group):
        arrived(buf.at[other], group + ("core",))

    def scatter_1(buf, from_y, group):
        for k in (2, 1, 3):
            j = lax.rem(y + k, 4)
            send(buf.at[pl.ds(4 * j, 4)], from_y.at[k - 1], group + ("y",), along_y(k))

    def scatter_2(buf, from_y, mid, from_z, group):
        total = buf[pl.ds(4 * y, 4)].astype(F32)
        arrived(from_y, group + ("y",))
        for k in range(3):
            total = total + from_y[k].astype(F32)
        mid[...] = total.astype(BF)
        for k in (2, 1, 3):
            send(mid.at[lax.rem(zl + k, 4)], from_z.at[k - 1], group + ("z",), along_z(k))

    def scatter_3(mid, from_z, group):
        total = mid[zl].astype(F32)
        arrived(from_z, group + ("z",))
        for k in range(3):
            total = total + from_z[k].astype(F32)
        return total

    def quad(g, j):
        return x_all.at[g, c, pl.ds(4 * j, 4)]

    def silu(v):
        return v / (1.0 + jnp.exp(-v))

    ones = jnp.ones((8, 448), BF)
    far_rows = pl.ds(pl.multiple_of((1 - zh) * 2 * RB, 2 * RB), 2 * RB)
    own_rows = pl.ds(pl.multiple_of(zh * 2 * RB, 2 * RB), 2 * RB)

    def out_rows(g):
        start = (g // SPLIT) * 32 + (g % SPLIT) * RB
        return slice(start, start + RB)

    def project(g):
        s, half = g // SPLIT, g % SPLIT
        if s not in gathered:
            gathered.append(s)
            gather_4(heads.at[s], ("heads", s))
        ordered = jnp.concatenate(
            [heads[s, n % 2, (n // 2 % 4) * 2 + n // 8] for n in range(16)], axis=0
        )
        by_request = dot(perm[half * span : (half + 1) * span, :], ordered).astype(BF)
        part[g] = dot_nt(by_request, w_out[...]).astype(BF).reshape(16, RB, 448)
        scatter_1(part.at[g], part_y.at[g], ("out", g))

    def project_2(g):
        scatter_2(part.at[g], part_y.at[g], part_mid.at[g], part_z.at[g], ("out", g))

    def residual(g):
        total = scatter_3(part_mid.at[g], part_z.at[g], ("out", g))
        x_all[g, c, t] = (hidden_ref[out_rows(g), :].astype(F32) + total).astype(BF)
        for k in (2, 1, 3):
            send(x_all.at[g, c, t], x_all.at[g, c, t], ("x", g, "z"), along_z(k))

    def spread_y(g):
        arrived(x_all.at[g, c, pl.ds(0, 3)], ("x", g, "z"))
        for k in (2, 1, 3):
            send(quad(g, y), quad(g, y), ("x", g, "y"), along_y(k))
        send(quad(g, y), quad(g, y), ("x", g, "core"), sibling)

    def spread_core(g):
        arrived(x_all.at[g, c, pl.ds(0, 12)], ("x", g, "y"))
        for k in range(1, 4):
            j = lax.rem(y + k, 4)
            send(quad(g, j), quad(g, j), ("x", g, "core"), sibling)

    def gate_up(g):
        arrived(x_all.at[g, other], ("x", g, "core"))
        rows = [x_all[g, core].reshape(16 * RB, 448) for core in range(2)]
        for n in range(3):
            cols = slice(n * 384, (n + 1) * 384)
            value = dot(rows[0], w_mix[0, :, cols]) + dot(rows[1], w_mix[1, :, cols])
            y_part[g, :, :, cols] = value.astype(BF).reshape(4, 4 * RB, 384)
        squares = jnp.zeros((8, 16 * RB), F32)
        for core in range(2):
            wide = rows[core].astype(F32)
            square = wide * wide
            high = square.astype(BF)
            squares = squares + dot_nt(ones, high) + dot_nt(ones, (square - high.astype(F32)).astype(BF))
        for n in range(8):
            s_part[g, n // 2, n % 2, :, 0 : 2 * RB] = squares[:, n * 2 * RB : (n + 1) * 2 * RB]
        for k in (2, 1, 3):
            j = lax.rem(x + k, 4)
            send(y_part.at[g, j], y_recv.at[g, k - 1], ("gate", g, "x"), along_x(k))
            send(s_part.at[g, j], s_recv.at[g, k - 1], ("gate", g, "xs"), along_x(k))

    def x_sum(g, rows):
        total = y_part[g, x, rows, :].astype(F32)
        for k in range(3):
            total = total + y_recv[g, k, rows, :].astype(F32)
        return total

    def s_sum(g, half):
        total = s_part[g, x, half]
        for k in range(3):
            total = total + s_recv[g, k, half]
        return total

    def gate_z(g):
        arrived(y_recv.at[g], ("gate", g, "x"))
        arrived(s_recv.at[g], ("gate", g, "xs"))
        y_mid[g] = x_sum(g, far_rows).astype(BF)
        s_mid[g] = s_sum(g, 1 - zh)
        send(y_mid.at[g], y_last.at[g], ("gate", g, "z"), z_partner)
        send(s_mid.at[g], s_last.at[g], ("gate", g, "zs"), z_partner)

    def activate(g):
        both = x_sum(g, own_rows)
        squares = s_sum(g, zh)
        arrived(y_last.at[g], ("gate", g, "z"))
        arrived(s_last.at[g], ("gate", g, "zs"))
        squares = (squares + s_last[g])[0:1, 0 : 2 * RB]
        inverse = lax.rsqrt(squares * (1.0 / D) + 1e-6)
        diagonal = iota((2 * RB, 2 * RB), 0) == iota((2 * RB, 2 * RB), 1)
        inverse = jnp.sum(jnp.where(diagonal, inverse, 0.0), axis=1, keepdims=True)
        both = (both + y_last[g].astype(F32)) * inverse
        acts[g, c, block, :, 0:512] = (silu(both[:, 0:512]) * both[:, 512:1024]).astype(BF)
        tail = both[:, 1024:1152]
        tail = jnp.where(
            iota((2 * RB, 128), 1) < 64, silu(tail) * pltpu.roll(tail, 64, 1), 0.0
        )
        acts[g, c, block, :, 512:640] = jnp.where(c == 0, tail, pltpu.roll(tail, 64, 1)).astype(BF)
        gather_1(acts.at[g], ("act", g))

    def act_x(g):
        gather_2(acts.at[g], ("act", g))

    def act_core(g):
        gather_3(acts.at[g], ("act", g))

    def descend(g):
        gather_4(acts.at[g], ("act", g))
        left = acts[g, 0].reshape(16 * RB, 640)
        right = acts[g, 1].reshape(16 * RB, 640)
        out = dot_nt(left[:, 0:512], w_down[:, 0:512]) + dot_nt(right[:, 0:512], w_down[:, 512:1024])
        out = out + dot_nt(left[:, 512:640] + right[:, 512:640], w_down[:, 1024:1152])
        down_part[g] = out.astype(BF).reshape(16, RB, 448)
        scatter_1(down_part.at[g], down_y.at[g], ("down", g))

    def descend_2(g):
        scatter_2(down_part.at[g], down_y.at[g], down_mid.at[g], down_z.at[g], ("down", g))

    def finish(g):
        if len(order) == 0:
            all_sent()
        fed = scatter_3(down_mid.at[g], down_z.at[g], ("down", g))
        o_ref[out_rows(g), :] = (x_all[g, c, t].astype(F32) + fed).astype(BF)

    def heads_x(s):
        gather_2(heads.at[s], ("heads", s))

    def heads_core(s):
        gather_3(heads.at[s], ("heads", s))

    stages = [
        project,
        project_2,
        residual,
        spread_y,
        spread_core,
        gate_up,
        gate_z,
        activate,
        act_x,
        act_core,
        descend,
        descend_2,
        finish,
    ]
    gathered = []
    order = list(ORDER)
    steps = {name: iter((head_outputs, heads_x, heads_core)) for name in "01"}
    steps.update({name: iter(stages) for name in "abcd"[:CHUNKS]})
    while order:
        name = order.pop(0)
        next(steps[name])("01".find(name) if name in "01" else "abcd".find(name))
    all_sent()


def on_device(
    q_nope,
    q_rope,
    cache_latent,
    cache_rope,
    cache_len,
    new_latent,
    new_rope,
    slot_request,
    w_uk,
    w_uv,
    w_out,
    hidden_state,
    norm_gain,
    w_gate,
    w_up,
    w_down,
):
    vmem = pl.BlockSpec(memory_space=pltpu.VMEM)
    anywhere = pl.BlockSpec(memory_space=pl.ANY)

    def buf(*shape, dtype=BF):
        return pltpu.VMEM(shape, dtype)

    out = pl.pallas_call(
        layer_kernel,
        out_shape=jax.ShapeDtypeStruct((64, 448), BF),
        in_specs=[pl.BlockSpec(memory_space=pltpu.SMEM), vmem, vmem] + [anywhere] * 13,
        out_specs=vmem,
        scratch_shapes=[
            buf(2, 2, 512),
            buf(2, 2, 64),
            buf(64, 448),
            buf(2, 2, 64, 128),
            buf(2, 2, 64, 64),
            buf(16, 16, 128),
            buf(16, 16, 128),
            buf(2, 16, 16, 256),
            buf(2, 16, 16, 256),
            buf(2, 16, 16, 256),
            buf(2, 16, 16, 256),
            buf(2, 2048, 512),
            buf(2, 64, 2048),
            buf(4, 128, 512),
            buf(4, 512, 128),
            buf(448, 512),
            buf(448, 1152),
            buf(2, 448, 1280),
            buf(2, 448, 1152),
            buf(2, 8, 448, dtype=F32),
            buf(512, 512),
            buf(256, 256),
            buf(2, 256, 256),
            buf(2, 128, 256),
            buf(2, 256, 128),
            buf(32, 128),
            buf(2, 2, 8, 32, 512),
            buf(CHUNKS, 16, RB, 448),
            buf(CHUNKS, 3, 4, RB, 448),
            buf(CHUNKS, 4, RB, 448),
            buf(CHUNKS, 3, RB, 448),
            buf(CHUNKS, 2, 16, RB, 448),
            buf(CHUNKS, 4, 4 * RB, 1152),
            buf(CHUNKS, 3, 4 * RB, 1152),
            buf(CHUNKS, 4, 2, 8, 128, dtype=F32),
            buf(CHUNKS, 3, 2, 8, 128, dtype=F32),
            buf(CHUNKS, 2 * RB, 1152),
            buf(CHUNKS, 2 * RB, 1152),
            buf(CHUNKS, 8, 128, dtype=F32),
            buf(CHUNKS, 8, 128, dtype=F32),
            buf(CHUNKS, 2, 8, 2 * RB, 640),
            buf(CHUNKS, 16, RB, 448),
            buf(CHUNKS, 3, 4, RB, 448),
            buf(CHUNKS, 4, RB, 448),
            buf(CHUNKS, 3, RB, 448),
            pltpu.SemaphoreType.DMA((15,)),
            pltpu.SemaphoreType.DMA((16 + 14 * CHUNKS,)),
            pltpu.SemaphoreType.DMA((16 + 14 * CHUNKS,)),
        ],
        compiler_params=pltpu.CompilerParams(
            collective_id=0, has_side_effects=True, vmem_limit_bytes=56 * 1024 * 1024
        ),
        name="layer",
    )(
        cache_len,
        slot_request.reshape(1, 512),
        norm_gain,
        new_latent,
        new_rope,
        hidden_state.reshape(64, 448),
        q_nope,
        q_rope,
        cache_latent,
        cache_rope,
        w_uk,
        w_uv,
        w_out.T,
        w_gate,
        w_up,
        w_down.T,
    )
    return out.reshape(2, 32, 448)


def solution(mesh):
    return jax.shard_map(
        on_device,
        mesh=mesh,
        in_specs=(
            P(None, ("dp", "tensor"), None, None),
            P(None, ("dp", "tensor"), None, None),
            P(("dp", "tensor"), None, None),
            P(("dp", "tensor"), None, None),
            P(("dp", "tensor")),
            P(None, ("dp", "tensor"), None),
            P(None, ("dp", "tensor"), None),
            P(),
            P("tensor", None, None),
            P("tensor", None, None),
            P("tensor", "dp"),
            P(None, "tensor", "dp"),
            P("dp"),
            P("dp", "tensor"),
            P("dp", "tensor"),
            P("tensor", "dp"),
        ),
        out_specs=P(None, "tensor", "dp"),
        check_vma=False,
    )
```

```python
import jax
import jax.numpy as jnp
from jax import lax
from jax.experimental import pallas as pl
from jax.experimental.pallas import tpu as pltpu
from jax.sharding import PartitionSpec as P

D = 7168
MESH = pl.DeviceIdType.MESH
BF = jnp.bfloat16
F32 = jnp.float32


def dot(a, b):
    return jnp.dot(a, b, preferred_element_type=F32)


def dot_nt(a, b):
    return lax.dot_general(a, b, (((1,), (1,)), ((), ())), preferred_element_type=F32)


def iota(shape, dim):
    return lax.broadcasted_iota(jnp.int32, shape, dim)


CHUNKS = 4
SPLIT = CHUNKS // 2
RB = 32 // SPLIT
ORDER = "".join(
    (
        "0010a1b1acbdabcadbcadaac",
        "abdabababacbccabadbcbcdd",
        "bcbcdcacddcdbdaddcabadcb",
        "bdccdadcbdabcd",
    )
)


def layer_kernel(
    len_ref,
    slot_ref,
    gain_ref,
    new_lat_hbm,
    new_rot_hbm,
    hidden_hbm,
    q_hbm,
    q_rot_hbm,
    lat_hbm,
    rot_hbm,
    uk_hbm,
    uv_hbm,
    out_hbm,
    gate_hbm,
    up_hbm,
    down_hbm,
    o_ref,
    new_lat_ref,
    new_rot_ref,
    hidden_ref,
    q_raw,
    q_rot_raw,
    q_send,
    q_recv,
    ql_send,
    ql_recv,
    ol_send,
    ol_recv,
    lat,
    rot,
    uk,
    uv,
    w_out,
    w_down,
    w_in,
    w_mix,
    gains,
    perm,
    by_block,
    picks,
    to_slots,
    to_blocks,
    pick,
    heads,
    part,
    part_y,
    part_mid,
    part_z,
    x_all,
    y_part,
    y_recv,
    y_far,
    y_pass,
    s_part,
    s_recv,
    y_mid,
    y_last,
    s_mid,
    s_last,
    acts,
    down_part,
    down_y,
    down_mid,
    down_z,
    local_sem,
    send_sem,
    recv_sem,
):
    d = lax.axis_index("dp")
    t = lax.axis_index("tensor")
    zh = lax.div(d, 8)
    x = lax.rem(lax.div(d, 2), 4)
    c = lax.rem(d, 2)
    y = lax.div(t, 4)
    zl = lax.rem(t, 4)
    other = 1 - c
    sibling = (d + 1 - 2 * c, t)
    z_partner = (lax.rem(d + 8, 16), t)
    block = x * 2 + zh
    far = x * 2 + 1 - zh

    def along_x(k):
        return (zh * 8 + lax.rem(x + k + 4, 4) * 2 + c, t)

    def along_y(k):
        return (d, lax.rem(y + k + 4, 4) * 4 + zl)

    def along_z(k):
        return (d, y * 4 + lax.rem(zl + k + 4, 4))

    sent = []
    groups = {}

    def remote(src, dst, group, device):
        n = groups.setdefault(group, len(groups))
        return pltpu.make_async_remote_copy(
            src_ref=src,
            dst_ref=dst,
            send_sem=send_sem.at[n],
            recv_sem=recv_sem.at[n],
            device_id=device,
            device_id_type=MESH,
        )

    def send(src, dst, group, device):
        remote(src, dst, group, device).start()

    def arrived(whole, group):
        remote(whole, whole, group, sibling).wait_recv()
        sent.append(remote(whole, whole, group, sibling))

    def all_sent():
        for copy in sent:
            copy.wait_send()
        sent.clear()

    def one_hot(ref, mask):
        ref[...] = jnp.where(mask, 1.0, 0.0).astype(BF)

    def load(src, dst, i):
        copy = pltpu.make_async_copy(src, dst, local_sem.at[i])
        copy.start()
        return copy

    barrier = pltpu.get_barrier_semaphore()
    for device in (z_partner, along_x(2), along_x(1), along_x(3), sibling):
        pl.semaphore_signal(barrier, inc=1, device_id=device, device_id_type=MESH)

    def greet(i, carry):
        pl.semaphore_signal(
            barrier, inc=1, device_id=(d, lax.rem(t + i, 16)), device_id_type=MESH
        )
        return carry

    lax.fori_loop(1, 16, greet, 0)

    load_q = load(q_hbm, q_raw, 0)
    load_uk = load(uk_hbm, uk, 1)
    load_q_rot = load(q_rot_hbm, q_rot_raw, 2)
    mine = pl.ds(pl.multiple_of(c * 512, 512), 512)
    load_in = [
        load(gate_hbm.at[:, mine], w_in.at[c, :, pl.ds(0, 512)], 3),
        load(up_hbm.at[:, mine], w_in.at[c, :, pl.ds(512, 512)], 4),
        load(gate_hbm.at[:, pl.ds(1024, 128)], w_in.at[c, :, pl.ds(1024, 128)], 5),
        load(up_hbm.at[:, pl.ds(1024, 128)], w_in.at[c, :, pl.ds(1152, 128)], 6),
    ]
    load_small = [
        load(new_lat_hbm, new_lat_ref, 12),
        load(new_rot_hbm, new_rot_ref, 13),
        load(hidden_hbm, hidden_ref, 14),
    ]
    load_lat = load(lat_hbm, lat, 7)
    load_rot = load(rot_hbm, rot, 8)
    load_uv = load(uv_hbm, uv, 9)
    load_out = load(out_hbm, w_out, 10)
    load_down = load(down_hbm, w_down, 11)

    row = iota((256, 256), 0)
    col = iota((256, 256), 1)
    source = ((row & 8) << 4) + ((row & 4) << 4) + ((row >> 4) << 2) + (row & 3)
    one_hot(by_block, col == source)
    for s in range(2):
        one_hot(picks.at[s], col == ((row >> 4) << 4) + 8 * s + (row & 7))
    def position(m, half):
        return ((m & 60) << 2) + half * 8 + ((m >> 6) << 2) + (m & 3)

    for half in range(2):
        one_hot(to_slots.at[half], iota((128, 256), 1) == position(iota((128, 256), 0), half))
        one_hot(to_blocks.at[half], iota((256, 128), 0) == position(iota((256, 128), 1), half))
    col = iota((32, 128), 1)
    one_hot(pick, (((col & 60) >> 1) + (col >> 6)) == iota((32, 128), 0))
    row = iota((512, 512), 0)
    span = 512 // SPLIT
    if SPLIT == 1:
        request = row
    else:
        request = ((row & 255) >> 4 << 5) + (row >> 8 << 4) + (row & 15)
    one_hot(perm, request == slot_ref[...])
    load_q.wait()
    q_send[...] = dot(by_block[...], q_raw[...].reshape(256, 128)).astype(BF).reshape(16, 16, 128)
    gains[c] = jnp.broadcast_to(gain_ref[...].astype(F32).reshape(1, 448), (8, 448))
    pl.semaphore_wait(barrier, 20)

    def exchange_start(src, dst, group):
        def one(i, carry):
            p = lax.rem(t + i, 16)
            send(src.at[p], dst.at[t], group, (d, p))
            return carry

        lax.fori_loop(1, 16, one, 0)
        dst[t] = src[t]

    def exchange_wait(dst, group):
        arrived(dst.at[pl.ds(0, 15)], group)

    exchange_start(q_send, q_recv, "q")

    theirs = pl.ds(pl.multiple_of(other * 512, 512), 512)
    send(gains.at[c], gains.at[c], ("w", 4), sibling)
    send(gate_hbm.at[:, theirs], w_in.at[c, :, pl.ds(0, 512)], ("w", 0), sibling)
    send(up_hbm.at[:, theirs], w_in.at[c, :, pl.ds(512, 512)], ("w", 1), sibling)
    send(gate_hbm.at[:, pl.ds(1024, 128)], w_in.at[c, :, pl.ds(1024, 128)], ("w", 2), sibling)
    send(up_hbm.at[:, pl.ds(1024, 128)], w_in.at[c, :, pl.ds(1152, 128)], ("w", 3), sibling)

    head_of_row = iota((256, 512), 0) & 3
    first_half = (iota((256, 256), 0) & 8) == 0
    load_uk.wait()
    exchange_wait(q_recv, "q")
    q_all = q_recv[...].reshape(256, 128)
    for s in range(2):
        q_rows = dot(picks[s], q_all).astype(BF)
        q_lat = jnp.zeros((256, 512), F32)
        for j in range(4):
            q_lat = jnp.where(head_of_row == j, dot(q_rows, uk[j]), q_lat)
        q_lat = jnp.where(first_half, q_lat[:, 0:256], q_lat[:, 256:512])
        ql_send[s] = q_lat.astype(BF).reshape(16, 16, 256)
        exchange_start(ql_send.at[s], ql_recv.at[s], ("ql", s))

    def slot_rows(blocks):
        blocks = blocks.reshape(256, 256)
        return jnp.concatenate([dot(to_slots[0], blocks), dot(to_slots[1], blocks)], axis=1)

    load_q_rot.wait()
    for copy in load_small:
        copy.wait()
    load_lat.wait()
    load_rot.wait()
    scale = 1.0 / 192.0**0.5
    for s in range(2):
        exchange_wait(ql_recv.at[s], ("ql", s))
        q_rows = slot_rows(ql_recv[s])
        results = []
        for r in range(2):
            q_wide = q_rows[64 * r : 64 * r + 64, :]
            q_turned = q_rot_raw[s, r]
            scores = (dot_nt(q_wide.astype(BF), lat[r]) + dot(q_turned, rot[r])) * scale
            scores = jnp.where(iota((64, 2048), 1) < len_ref[r], scores, -1e30)
            q_turned_wide = q_turned.astype(F32)
            top = jnp.max(scores, axis=1, keepdims=True)
            fresh = []
            for u in range(s + 1):
                value = jnp.sum(
                    q_wide * new_lat_ref[u, r : r + 1, :].astype(F32), axis=1, keepdims=True
                )
                value = value + jnp.sum(
                    q_turned_wide * new_rot_ref[u, r : r + 1, :].astype(F32), axis=1, keepdims=True
                )
                value = value * scale
                top = jnp.maximum(top, value)
                fresh.append(value)
            weights = jnp.exp(scores - top)
            total = jnp.sum(weights, axis=1, keepdims=True)
            mixed = dot(weights.astype(BF), lat[r])
            for u in range(s + 1):
                weight = jnp.exp(fresh[u] - top)
                total = total + weight
                mixed = mixed + weight * new_lat_ref[u, r : r + 1, :].astype(F32)
            results.append((mixed / total).astype(BF))
        mixed = jnp.concatenate(results, axis=0)
        mixed = dot(to_blocks[0], mixed[:, 0:256]) + dot(to_blocks[1], mixed[:, 256:512])
        ol_send[s] = mixed.astype(BF).reshape(16, 16, 256)
        exchange_start(ol_send.at[s], ol_recv.at[s], ("ol", s))

    for copy in load_in:
        copy.wait()
    arrived(w_in.at[other, :, pl.ds(0, 512)], ("w", 0))
    arrived(w_in.at[other, :, pl.ds(512, 512)], ("w", 1))
    arrived(w_in.at[other, :, pl.ds(1024, 128)], ("w", 2))
    arrived(w_in.at[other, :, pl.ds(1152, 128)], ("w", 3))
    arrived(gains.at[other], ("w", 4))
    low = iota((448, 128), 1) < 64
    eye = iota((448, 448), 0) == iota((448, 448), 1)
    for k in range(2):
        gain = jnp.sum(jnp.where(eye, gains[k, 0:1, :], 0.0), axis=1, keepdims=True)
        for j in range(8):
            cols = pl.ds(j * 128, 128)
            w_mix[k, :, cols] = (w_in[k, :, cols].astype(F32) * gain).astype(BF)
        gate_tail = w_in[k, :, pl.ds(1024, 128)].astype(F32)
        up_tail = w_in[k, :, pl.ds(1152, 128)].astype(F32)
        first = jnp.where(low, gate_tail, pltpu.roll(up_tail, 64, 1))
        second = jnp.where(low, pltpu.roll(gate_tail, 64, 1), up_tail)
        tail = jnp.where(c == 0, first, second)
        w_mix[k, :, pl.ds(1024, 128)] = (tail * gain).astype(BF)

    load_uv.wait()
    load_out.wait()
    load_down.wait()
    own_head = iota((128, 128), 0) & 3

    def head_outputs(s):
        exchange_wait(ol_recv.at[s], ("ol", s))
        o_rows = slot_rows(ol_recv[s]).astype(BF)
        spread = [jnp.where(own_head == j, dot(o_rows, uv[j]), 0.0).astype(BF) for j in range(4)]
        heads[s, c, block] = dot(pick[...], jnp.concatenate(spread, axis=1)).astype(BF)
        gather_1(heads.at[s], ("heads", s))

    def gather_send(buf, b, group):
        for k in (2, 1, 3):
            send(buf.at[c, b], buf.at[c, b], group, along_x(k))

    def gather_1(buf, group):
        send(buf.at[c, block], buf.at[c, block], group + ("z",), z_partner)
        gather_send(buf, block, group + ("x",))

    def pair(buf, j):
        return buf.at[c, pl.ds(2 * j, 2)]

    def gather_2(buf, group):
        arrived(buf.at[c, far], group + ("z",))
        gather_send(buf, far, group + ("xz",))
        send(pair(buf, x), pair(buf, x), group + ("core",), sibling)

    def gather_3(buf, group):
        arrived(buf.at[c, pl.ds(0, 3)], group + ("x",))
        arrived(buf.at[c, pl.ds(0, 3)], group + ("xz",))
        for k in range(1, 4):
            j = lax.rem(x + k, 4)
            send(pair(buf, j), pair(buf, j), group + ("core",), sibling)

    def gather_4(buf, group):
        arrived(buf.at[other], group + ("core",))

    def scatter_1(buf, from_y, group):
        for k in (2, 1, 3):
            j = lax.rem(y + k, 4)
            send(buf.at[pl.ds(4 * j, 4)], from_y.at[k - 1], group + ("y",), along_y(k))

    def scatter_2(buf, from_y, mid, from_z, group):
        total = buf[pl.ds(4 * y, 4)].astype(F32)
        arrived(from_y, group + ("y",))
        for k in range(3):
            total = total + from_y[k].astype(F32)
        mid[...] = total.astype(BF)
        for k in (2, 1, 3):
            send(mid.at[lax.rem(zl + k, 4)], from_z.at[k - 1], group + ("z",), along_z(k))

    def scatter_3(mid, from_z, group):
        total = mid[zl].astype(F32)
        arrived(from_z, group + ("z",))
        for k in range(3):
            total = total + from_z[k].astype(F32)
        return total

    def quad(g, j):
        return x_all.at[g, c, pl.ds(4 * j, 4)]

    def silu(v):
        return v / (1.0 + jnp.exp(-v))

    ones = jnp.ones((8, 448), BF)
    low_rows = pl.ds(0, 2 * RB)
    high_rows = pl.ds(2 * RB, 2 * RB)
    far_rows = pl.ds(pl.multiple_of((1 - zh) * 2 * RB, 2 * RB), 2 * RB)
    own_rows = pl.ds(pl.multiple_of(zh * 2 * RB, 2 * RB), 2 * RB)

    def out_rows(g):
        start = (g // SPLIT) * 32 + (g % SPLIT) * RB
        return slice(start, start + RB)

    def project(g):
        s, half = g // SPLIT, g % SPLIT
        if s not in gathered:
            gathered.append(s)
            gather_4(heads.at[s], ("heads", s))
        ordered = jnp.concatenate(
            [heads[s, n % 2, (n // 2 % 4) * 2 + n // 8] for n in range(16)], axis=0
        )
        by_request = dot(perm[half * span : (half + 1) * span, :], ordered).astype(BF)
        part[g] = dot_nt(by_request, w_out[...]).astype(BF).reshape(16, RB, 448)
        scatter_1(part.at[g], part_y.at[g], ("out", g))

    def project_2(g):
        scatter_2(part.at[g], part_y.at[g], part_mid.at[g], part_z.at[g], ("out", g))

    def residual(g):
        total = scatter_3(part_mid.at[g], part_z.at[g], ("out", g))
        x_all[g, c, t] = (hidden_ref[out_rows(g), :].astype(F32) + total).astype(BF)
        for k in (2, 1, 3):
            send(x_all.at[g, c, t], x_all.at[g, c, t], ("x", g, "z"), along_z(k))

    def spread_y(g):
        arrived(x_all.at[g, c, pl.ds(0, 3)], ("x", g, "z"))
        for k in (2, 1, 3):
            send(quad(g, y), quad(g, y), ("x", g, "y"), along_y(k))
        send(quad(g, y), quad(g, y), ("x", g, "core"), sibling)

    def spread_core(g):
        arrived(x_all.at[g, c, pl.ds(0, 12)], ("x", g, "y"))
        for k in range(1, 4):
            j = lax.rem(y + k, 4)
            send(quad(g, j), quad(g, j), ("x", g, "core"), sibling)

    def gate_up(g):
        arrived(x_all.at[g, other], ("x", g, "core"))

    def gate_part(g, p):
        rows = [x_all[g, core].reshape(16 * RB, 448) for core in range(2)]
        cols = slice(p * 384, (p + 1) * 384)
        value = dot(rows[0], w_mix[0, :, cols]) + dot(rows[1], w_mix[1, :, cols])
        y_part[g, p] = value.astype(BF).reshape(4, 4 * RB, 384)
        after, before, away = (lax.rem(x + k, 4) for k in (1, 3, 2))
        send(y_part.at[g, p, away, low_rows], y_far.at[g, p, 0], ("gate", g, "far", p), along_x(1))
        send(y_part.at[g, p, away, high_rows], y_far.at[g, p, 1], ("gate", g, "far", p), along_x(3))
        group = ("gate", g, "x", p)
        send(y_part.at[g, p, after, high_rows], y_recv.at[g, p, 0, high_rows], group, along_x(1))
        send(y_part.at[g, p, before, low_rows], y_recv.at[g, p, 1, low_rows], group, along_x(3))

    def pass_on(g, p):
        arrived(y_far.at[g, p], ("gate", g, "far", p))
        after, before = (lax.rem(x + k, 4) for k in (1, 3))
        group = ("gate", g, "x", p)
        total = y_part[g, p, after, low_rows, :].astype(F32) + y_far[g, p, 0].astype(F32)
        y_pass[g, p, 0] = total.astype(BF)
        send(y_pass.at[g, p, 0], y_recv.at[g, p, 0, low_rows], group, along_x(1))
        total = y_part[g, p, before, high_rows, :].astype(F32) + y_far[g, p, 1].astype(F32)
        y_pass[g, p, 1] = total.astype(BF)
        send(y_pass.at[g, p, 1], y_recv.at[g, p, 1, high_rows], group, along_x(3))

    def pass_on_0(g):
        pass_on(g, 0)

    def pass_on_1(g):
        pass_on(g, 1)

    def pass_on_2(g):
        pass_on(g, 2)

    def gate_up_0(g):
        gate_up(g)
        gate_part(g, 0)

    def gate_up_1(g):
        gate_part(g, 1)

    def gate_up_2(g):
        gate_part(g, 2)
        squares = jnp.zeros((8, 16 * RB), F32)
        for core in range(2):
            wide = x_all[g, core].reshape(16 * RB, 448).astype(F32)
            square = wide * wide
            high = square.astype(BF)
            squares = squares + dot_nt(ones, high) + dot_nt(ones, (square - high.astype(F32)).astype(BF))
        for n in range(8):
            s_part[g, n // 2, n % 2, :, 0 : 2 * RB] = squares[:, n * 2 * RB : (n + 1) * 2 * RB]
        for k in (2, 1, 3):
            j = lax.rem(x + k, 4)
            send(s_part.at[g, j], s_recv.at[g, k - 1], ("gate", g, "xs"), along_x(k))

    def x_sum(g, p, rows):
        total = y_part[g, p, x, rows, :].astype(F32)
        for k in range(2):
            total = total + y_recv[g, p, k, rows, :].astype(F32)
        return total

    def s_sum(g, half):
        total = s_part[g, x, half]
        for k in range(3):
            total = total + s_recv[g, k, half]
        return total

    def gate_z(g, p):
        arrived(y_recv.at[g, p], ("gate", g, "x", p))
        y_mid[g, p] = x_sum(g, p, far_rows).astype(BF)
        send(y_mid.at[g, p], y_last.at[g, p], ("gate", g, "z", p), z_partner)

    def gate_z_0(g):
        gate_z(g, 0)

    def gate_z_1(g):
        gate_z(g, 1)

    def gate_z_2(g):
        gate_z(g, 2)
        arrived(s_recv.at[g], ("gate", g, "xs"))
        s_mid[g] = s_sum(g, 1 - zh)
        send(s_mid.at[g], s_last.at[g], ("gate", g, "zs"), z_partner)

    def activate(g):
        parts = [x_sum(g, p, own_rows) for p in range(3)]
        squares = s_sum(g, zh)
        for p in range(3):
            arrived(y_last.at[g, p], ("gate", g, "z", p))
        arrived(s_last.at[g], ("gate", g, "zs"))
        squares = (squares + s_last[g])[0:1, 0 : 2 * RB]
        inverse = lax.rsqrt(squares * (1.0 / D) + 1e-6)
        diagonal = iota((2 * RB, 2 * RB), 0) == iota((2 * RB, 2 * RB), 1)
        inverse = jnp.sum(jnp.where(diagonal, inverse, 0.0), axis=1, keepdims=True)
        parts = [parts[p] + y_last[g, p].astype(F32) for p in range(3)]
        both = jnp.concatenate(parts, axis=1) * inverse
        acts[g, c, block, :, 0:512] = (silu(both[:, 0:512]) * both[:, 512:1024]).astype(BF)
        tail = both[:, 1024:1152]
        tail = jnp.where(
            iota((2 * RB, 128), 1) < 64, silu(tail) * pltpu.roll(tail, 64, 1), 0.0
        )
        acts[g, c, block, :, 512:640] = jnp.where(c == 0, tail, pltpu.roll(tail, 64, 1)).astype(BF)
        gather_1(acts.at[g], ("act", g))

    def act_x(g):
        gather_2(acts.at[g], ("act", g))

    def act_core(g):
        gather_3(acts.at[g], ("act", g))

    def descend(g):
        gather_4(acts.at[g], ("act", g))
        left = acts[g, 0].reshape(16 * RB, 640)
        right = acts[g, 1].reshape(16 * RB, 640)
        out = dot_nt(left[:, 0:512], w_down[:, 0:512]) + dot_nt(right[:, 0:512], w_down[:, 512:1024])
        out = out + dot_nt(left[:, 512:640] + right[:, 512:640], w_down[:, 1024:1152])
        down_part[g] = out.astype(BF).reshape(16, RB, 448)
        scatter_1(down_part.at[g], down_y.at[g], ("down", g))

    def descend_2(g):
        scatter_2(down_part.at[g], down_y.at[g], down_mid.at[g], down_z.at[g], ("down", g))

    def finish(g):
        if len(order) == 0:
            all_sent()
        fed = scatter_3(down_mid.at[g], down_z.at[g], ("down", g))
        o_ref[out_rows(g), :] = (x_all[g, c, t].astype(F32) + fed).astype(BF)

    def heads_x(s):
        gather_2(heads.at[s], ("heads", s))

    def heads_core(s):
        gather_3(heads.at[s], ("heads", s))

    stages = [
        project,
        project_2,
        residual,
        spread_y,
        spread_core,
        gate_up_0,
        gate_up_1,
        gate_up_2,
        pass_on_0,
        pass_on_1,
        pass_on_2,
        gate_z_0,
        gate_z_1,
        gate_z_2,
        activate,
        act_x,
        act_core,
        descend,
        descend_2,
        finish,
    ]
    gathered = []
    order = list(ORDER)
    steps = {name: iter((head_outputs, heads_x, heads_core)) for name in "01"}
    steps.update({name: iter(stages) for name in "abcd"[:CHUNKS]})
    while order:
        name = order.pop(0)
        next(steps[name])("01".find(name) if name in "01" else "abcd".find(name))
    all_sent()


def on_device(
    q_nope,
    q_rope,
    cache_latent,
    cache_rope,
    cache_len,
    new_latent,
    new_rope,
    slot_request,
    w_uk,
    w_uv,
    w_out,
    hidden_state,
    norm_gain,
    w_gate,
    w_up,
    w_down,
):
    vmem = pl.BlockSpec(memory_space=pltpu.VMEM)
    anywhere = pl.BlockSpec(memory_space=pl.ANY)

    def buf(*shape, dtype=BF):
        return pltpu.VMEM(shape, dtype)

    out = pl.pallas_call(
        layer_kernel,
        out_shape=jax.ShapeDtypeStruct((64, 448), BF),
        in_specs=[pl.BlockSpec(memory_space=pltpu.SMEM), vmem, vmem] + [anywhere] * 13,
        out_specs=vmem,
        scratch_shapes=[
            buf(2, 2, 512),
            buf(2, 2, 64),
            buf(64, 448),
            buf(2, 2, 64, 128),
            buf(2, 2, 64, 64),
            buf(16, 16, 128),
            buf(16, 16, 128),
            buf(2, 16, 16, 256),
            buf(2, 16, 16, 256),
            buf(2, 16, 16, 256),
            buf(2, 16, 16, 256),
            buf(2, 2048, 512),
            buf(2, 64, 2048),
            buf(4, 128, 512),
            buf(4, 512, 128),
            buf(448, 512),
            buf(448, 1152),
            buf(2, 448, 1280),
            buf(2, 448, 1152),
            buf(2, 8, 448, dtype=F32),
            buf(512, 512),
            buf(256, 256),
            buf(2, 256, 256),
            buf(2, 128, 256),
            buf(2, 256, 128),
            buf(32, 128),
            buf(2, 2, 8, 32, 512),
            buf(CHUNKS, 16, RB, 448),
            buf(CHUNKS, 3, 4, RB, 448),
            buf(CHUNKS, 4, RB, 448),
            buf(CHUNKS, 3, RB, 448),
            buf(CHUNKS, 2, 16, RB, 448),
            buf(CHUNKS, 3, 4, 4 * RB, 384),
            buf(CHUNKS, 3, 2, 4 * RB, 384),
            buf(CHUNKS, 3, 2, 2 * RB, 384),
            buf(CHUNKS, 3, 2, 2 * RB, 384),
            buf(CHUNKS, 4, 2, 8, 128, dtype=F32),
            buf(CHUNKS, 3, 2, 8, 128, dtype=F32),
            buf(CHUNKS, 3, 2 * RB, 384),
            buf(CHUNKS, 3, 2 * RB, 384),
            buf(CHUNKS, 8, 128, dtype=F32),
            buf(CHUNKS, 8, 128, dtype=F32),
            buf(CHUNKS, 2, 8, 2 * RB, 640),
            buf(CHUNKS, 16, RB, 448),
            buf(CHUNKS, 3, 4, RB, 448),
            buf(CHUNKS, 4, RB, 448),
            buf(CHUNKS, 3, RB, 448),
            pltpu.SemaphoreType.DMA((15,)),
            pltpu.SemaphoreType.DMA((18 + 22 * CHUNKS,)),
            pltpu.SemaphoreType.DMA((18 + 22 * CHUNKS,)),
        ],
        compiler_params=pltpu.CompilerParams(
            collective_id=0, has_side_effects=True, vmem_limit_bytes=56 * 1024 * 1024
        ),
        name="layer",
    )(
        cache_len,
        slot_request.reshape(1, 512),
        norm_gain,
        new_latent,
        new_rope,
        hidden_state.reshape(64, 448),
        q_nope,
        q_rope,
        cache_latent,
        cache_rope,
        w_uk,
        w_uv,
        w_out.T,
        w_gate,
        w_up,
        w_down.T,
    )
    return out.reshape(2, 32, 448)


def solution(mesh):
    return jax.shard_map(
        on_device,
        mesh=mesh,
        in_specs=(
            P(None, ("dp", "tensor"), None, None),
            P(None, ("dp", "tensor"), None, None),
            P(("dp", "tensor"), None, None),
            P(("dp", "tensor"), None, None),
            P(("dp", "tensor")),
            P(None, ("dp", "tensor"), None),
            P(None, ("dp", "tensor"), None),
            P(),
            P("tensor", None, None),
            P("tensor", None, None),
            P("tensor", "dp"),
            P(None, "tensor", "dp"),
            P("dp"),
            P("dp", "tensor"),
            P("dp", "tensor"),
            P("tensor", "dp"),
        ),
        out_specs=P(None, "tensor", "dp"),
        check_vma=False,
    )
```

```python
import jax
import jax.numpy as jnp
from jax import lax
from jax.experimental import pallas as pl
from jax.experimental.pallas import tpu as pltpu
from jax.sharding import PartitionSpec as P

D = 7168
MESH = pl.DeviceIdType.MESH
BF = jnp.bfloat16
F32 = jnp.float32


def dot(a, b):
    return jnp.dot(a, b, preferred_element_type=F32)


def dot_nt(a, b):
    return lax.dot_general(a, b, (((1,), (1,)), ((), ())), preferred_element_type=F32)


def iota(shape, dim):
    return lax.broadcasted_iota(jnp.int32, shape, dim)


CHUNKS = 4
SPLIT = CHUNKS // 2
RB = 32 // SPLIT
ORDER = "".join(
    (
        "0010b1a1bdacbdabcdabcbdb",
        "bacbabadbaadbbcadabdadca",
        "cdadcdbcddccacbccdbacadb",
        "acddcacbdcbdac",
    )
)


def layer_kernel(
    len_ref,
    slot_ref,
    gain_ref,
    new_lat_hbm,
    new_rot_hbm,
    hidden_hbm,
    q_hbm,
    q_rot_hbm,
    lat_hbm,
    rot_hbm,
    uk_hbm,
    uv_hbm,
    out_hbm,
    gate_hbm,
    up_hbm,
    down_hbm,
    o_ref,
    new_lat_ref,
    new_rot_ref,
    hidden_ref,
    q_raw,
    q_rot_raw,
    q_send,
    q_recv,
    ql_send,
    ql_recv,
    ol_send,
    ol_recv,
    lat,
    rot,
    uk,
    uv,
    w_out,
    w_down,
    w_in,
    w_mix,
    gains,
    perm,
    by_block,
    picks,
    to_slots,
    to_blocks,
    pick,
    heads,
    part,
    part_y,
    part_mid,
    part_z,
    x_all,
    y_part,
    y_recv,
    y_far,
    y_pass,
    s_part,
    s_recv,
    y_mid,
    y_last,
    s_mid,
    s_last,
    acts,
    down_part,
    down_y,
    down_mid,
    down_z,
    local_sem,
    send_sem,
    recv_sem,
):
    d = lax.axis_index("dp")
    t = lax.axis_index("tensor")
    zh = lax.div(d, 8)
    x = lax.rem(lax.div(d, 2), 4)
    c = lax.rem(d, 2)
    y = lax.div(t, 4)
    zl = lax.rem(t, 4)
    other = 1 - c
    sibling = (d + 1 - 2 * c, t)
    z_partner = (lax.rem(d + 8, 16), t)
    block = x * 2 + zh
    far = x * 2 + 1 - zh

    def along_x(k):
        return (zh * 8 + lax.rem(x + k + 4, 4) * 2 + c, t)

    def along_y(k):
        return (d, lax.rem(y + k + 4, 4) * 4 + zl)

    def along_z(k):
        return (d, y * 4 + lax.rem(zl + k + 4, 4))

    sent = []
    groups = {}

    def remote(src, dst, group, device):
        n = groups.setdefault(group, len(groups))
        return pltpu.make_async_remote_copy(
            src_ref=src,
            dst_ref=dst,
            send_sem=send_sem.at[n],
            recv_sem=recv_sem.at[n],
            device_id=device,
            device_id_type=MESH,
        )

    def send(src, dst, group, device):
        remote(src, dst, group, device).start()

    def arrived(whole, group):
        remote(whole, whole, group, sibling).wait_recv()
        sent.append(remote(whole, whole, group, sibling))

    def all_sent():
        for copy in sent:
            copy.wait_send()
        sent.clear()

    def one_hot(ref, mask):
        ref[...] = jnp.where(mask, 1.0, 0.0).astype(BF)

    def load(src, dst, i):
        copy = pltpu.make_async_copy(src, dst, local_sem.at[i])
        copy.start()
        return copy

    barrier = pltpu.get_barrier_semaphore()
    for device in (z_partner, along_x(2), along_x(1), along_x(3), sibling):
        pl.semaphore_signal(barrier, inc=1, device_id=device, device_id_type=MESH)

    def greet(i, carry):
        pl.semaphore_signal(
            barrier, inc=1, device_id=(d, lax.rem(t + i, 16)), device_id_type=MESH
        )
        return carry

    lax.fori_loop(1, 16, greet, 0)

    load_q = load(q_hbm, q_raw, 0)
    load_uk = load(uk_hbm, uk, 1)
    load_q_rot = load(q_rot_hbm, q_rot_raw, 2)
    mine = pl.ds(pl.multiple_of(c * 512, 512), 512)
    load_in = [
        load(gate_hbm.at[:, mine], w_in.at[c, :, pl.ds(0, 512)], 3),
        load(up_hbm.at[:, mine], w_in.at[c, :, pl.ds(512, 512)], 4),
        load(gate_hbm.at[:, pl.ds(1024, 128)], w_in.at[c, :, pl.ds(1024, 128)], 5),
        load(up_hbm.at[:, pl.ds(1024, 128)], w_in.at[c, :, pl.ds(1152, 128)], 6),
    ]
    load_small = [
        load(new_lat_hbm, new_lat_ref, 12),
        load(new_rot_hbm, new_rot_ref, 13),
        load(hidden_hbm, hidden_ref, 14),
    ]
    load_lat = load(lat_hbm, lat, 7)
    load_rot = load(rot_hbm, rot, 8)
    load_uv = load(uv_hbm, uv, 9)
    load_out = load(out_hbm, w_out, 10)
    load_down = load(down_hbm, w_down, 11)

    row = iota((256, 256), 0)
    col = iota((256, 256), 1)
    source = ((row & 8) << 4) + ((row & 4) << 4) + ((row >> 4) << 2) + (row & 3)
    one_hot(by_block, col == source)
    for s in range(2):
        one_hot(picks.at[s], col == ((row >> 4) << 4) + 8 * s + (row & 7))
    def position(m, half):
        return ((m & 60) << 2) + half * 8 + ((m >> 6) << 2) + (m & 3)

    for half in range(2):
        one_hot(to_slots.at[half], iota((128, 256), 1) == position(iota((128, 256), 0), half))
        one_hot(to_blocks.at[half], iota((256, 128), 0) == position(iota((256, 128), 1), half))
    col = iota((32, 128), 1)
    one_hot(pick, (((col & 60) >> 1) + (col >> 6)) == iota((32, 128), 0))
    row = iota((512, 512), 0)
    span = 512 // SPLIT
    if SPLIT == 1:
        request = row
    else:
        request = ((row & 255) >> 4 << 5) + (row >> 8 << 4) + (row & 15)
    one_hot(perm, request == slot_ref[...])
    load_q.wait()
    q_send[...] = dot(by_block[...], q_raw[...].reshape(256, 128)).astype(BF).reshape(16, 16, 128)
    gains[c] = jnp.broadcast_to(gain_ref[...].astype(F32).reshape(1, 448), (8, 448))
    pl.semaphore_wait(barrier, 20)

    def exchange_start(src, dst, group):
        def one(i, carry):
            p = lax.rem(t + i, 16)
            send(src.at[p], dst.at[t], group, (d, p))
            return carry

        lax.fori_loop(1, 16, one, 0)
        dst[t] = src[t]

    def exchange_wait(dst, group):
        arrived(dst.at[pl.ds(0, 15)], group)

    exchange_start(q_send, q_recv, "q")

    theirs = pl.ds(pl.multiple_of(other * 512, 512), 512)
    send(gains.at[c], gains.at[c], ("w", 4), sibling)
    send(gate_hbm.at[:, theirs], w_in.at[c, :, pl.ds(0, 512)], ("w", 0), sibling)
    send(up_hbm.at[:, theirs], w_in.at[c, :, pl.ds(512, 512)], ("w", 1), sibling)
    send(gate_hbm.at[:, pl.ds(1024, 128)], w_in.at[c, :, pl.ds(1024, 128)], ("w", 2), sibling)
    send(up_hbm.at[:, pl.ds(1024, 128)], w_in.at[c, :, pl.ds(1152, 128)], ("w", 3), sibling)

    head_of_row = iota((256, 512), 0) & 3
    first_half = (iota((256, 256), 0) & 8) == 0
    load_uk.wait()
    exchange_wait(q_recv, "q")
    q_all = q_recv[...].reshape(256, 128)
    for s in range(2):
        q_rows = dot(picks[s], q_all).astype(BF)
        q_lat = jnp.zeros((256, 512), F32)
        for j in range(4):
            q_lat = jnp.where(head_of_row == j, dot(q_rows, uk[j]), q_lat)
        q_lat = jnp.where(first_half, q_lat[:, 0:256], q_lat[:, 256:512])
        ql_send[s] = q_lat.astype(BF).reshape(16, 16, 256)
        exchange_start(ql_send.at[s], ql_recv.at[s], ("ql", s))

    def slot_rows(blocks):
        blocks = blocks.reshape(256, 256)
        return jnp.concatenate([dot(to_slots[0], blocks), dot(to_slots[1], blocks)], axis=1)

    load_q_rot.wait()
    for copy in load_small:
        copy.wait()
    load_lat.wait()
    load_rot.wait()
    scale = 1.0 / 192.0**0.5
    for s in range(2):
        exchange_wait(ql_recv.at[s], ("ql", s))
        q_rows = slot_rows(ql_recv[s])
        results = []
        for r in range(2):
            q_wide = q_rows[64 * r : 64 * r + 64, :]
            q_turned = q_rot_raw[s, r]
            scores = (dot_nt(q_wide.astype(BF), lat[r]) + dot(q_turned, rot[r])) * scale
            scores = jnp.where(iota((64, 2048), 1) < len_ref[r], scores, -1e30)
            q_turned_wide = q_turned.astype(F32)
            top = jnp.max(scores, axis=1, keepdims=True)
            fresh = []
            for u in range(s + 1):
                value = jnp.sum(
                    q_wide * new_lat_ref[u, r : r + 1, :].astype(F32), axis=1, keepdims=True
                )
                value = value + jnp.sum(
                    q_turned_wide * new_rot_ref[u, r : r + 1, :].astype(F32), axis=1, keepdims=True
                )
                value = value * scale
                top = jnp.maximum(top, value)
                fresh.append(value)
            weights = jnp.exp(scores - top)
            total = jnp.sum(weights, axis=1, keepdims=True)
            mixed = dot(weights.astype(BF), lat[r])
            for u in range(s + 1):
                weight = jnp.exp(fresh[u] - top)
                total = total + weight
                mixed = mixed + weight * new_lat_ref[u, r : r + 1, :].astype(F32)
            results.append((mixed / total).astype(BF))
        mixed = jnp.concatenate(results, axis=0)
        mixed = dot(to_blocks[0], mixed[:, 0:256]) + dot(to_blocks[1], mixed[:, 256:512])
        ol_send[s] = mixed.astype(BF).reshape(16, 16, 256)
        exchange_start(ol_send.at[s], ol_recv.at[s], ("ol", s))

    for copy in load_in:
        copy.wait()
    arrived(w_in.at[other, :, pl.ds(0, 512)], ("w", 0))
    arrived(w_in.at[other, :, pl.ds(512, 512)], ("w", 1))
    arrived(w_in.at[other, :, pl.ds(1024, 128)], ("w", 2))
    arrived(w_in.at[other, :, pl.ds(1152, 128)], ("w", 3))
    arrived(gains.at[other], ("w", 4))
    low = iota((448, 128), 1) < 64
    eye = iota((448, 448), 0) == iota((448, 448), 1)
    for k in range(2):
        gain = jnp.sum(jnp.where(eye, gains[k, 0:1, :], 0.0), axis=1, keepdims=True)
        for j in range(8):
            cols = pl.ds(j * 128, 128)
            w_mix[k, :, cols] = (w_in[k, :, cols].astype(F32) * gain).astype(BF)
        gate_tail = w_in[k, :, pl.ds(1024, 128)].astype(F32)
        up_tail = w_in[k, :, pl.ds(1152, 128)].astype(F32)
        first = jnp.where(low, gate_tail, pltpu.roll(up_tail, 64, 1))
        second = jnp.where(low, pltpu.roll(gate_tail, 64, 1), up_tail)
        tail = jnp.where(c == 0, first, second)
        w_mix[k, :, pl.ds(1024, 128)] = (tail * gain).astype(BF)

    load_uv.wait()
    load_out.wait()
    load_down.wait()
    own_head = iota((128, 128), 0) & 3

    def head_outputs(s):
        exchange_wait(ol_recv.at[s], ("ol", s))
        o_rows = slot_rows(ol_recv[s]).astype(BF)
        spread = [jnp.where(own_head == j, dot(o_rows, uv[j]), 0.0).astype(BF) for j in range(4)]
        heads[s, c, block] = dot(pick[...], jnp.concatenate(spread, axis=1)).astype(BF)
        gather_1(heads.at[s], ("heads", s))

    def gather_send(buf, b, group):
        for k in (2, 1, 3):
            send(buf.at[c, b], buf.at[c, b], group, along_x(k))

    def gather_1(buf, group):
        send(buf.at[c, block], buf.at[c, block], group + ("z",), z_partner)
        gather_send(buf, block, group + ("x",))

    def pair(buf, j):
        return buf.at[c, pl.ds(2 * j, 2)]

    def gather_2(buf, group):
        arrived(buf.at[c, far], group + ("z",))
        gather_send(buf, far, group + ("xz",))
        send(pair(buf, x), pair(buf, x), group + ("core",), sibling)

    def gather_3(buf, group):
        arrived(buf.at[c, pl.ds(0, 3)], group + ("x",))
        arrived(buf.at[c, pl.ds(0, 3)], group + ("xz",))
        for k in range(1, 4):
            j = lax.rem(x + k, 4)
            send(pair(buf, j), pair(buf, j), group + ("core",), sibling)

    def gather_4(buf, group):
        arrived(buf.at[other], group + ("core",))

    def scatter_1(buf, from_y, group):
        for k in (2, 1, 3):
            j = lax.rem(y + k, 4)
            send(buf.at[pl.ds(4 * j, 4)], from_y.at[k - 1], group + ("y",), along_y(k))

    def scatter_2(buf, from_y, mid, from_z, group):
        total = buf[pl.ds(4 * y, 4)].astype(F32)
        arrived(from_y, group + ("y",))
        for k in range(3):
            total = total + from_y[k].astype(F32)
        mid[...] = total.astype(BF)
        for k in (2, 1, 3):
            send(mid.at[lax.rem(zl + k, 4)], from_z.at[k - 1], group + ("z",), along_z(k))

    def scatter_3(mid, from_z, group):
        total = mid[zl].astype(F32)
        arrived(from_z, group + ("z",))
        for k in range(3):
            total = total + from_z[k].astype(F32)
        return total

    def quad(g, j):
        return x_all.at[g, c, pl.ds(4 * j, 4)]

    def silu(v):
        return v / (1.0 + jnp.exp(-v))

    lane = iota((8, 128), 1)
    sum_lanes = jnp.where((lane >= 64) & (lane < 67), 1.0, 0.0).astype(BF)
    low_rows = pl.ds(0, 2 * RB)
    high_rows = pl.ds(2 * RB, 2 * RB)
    far_rows = pl.ds(pl.multiple_of((1 - zh) * 2 * RB, 2 * RB), 2 * RB)
    own_rows = pl.ds(pl.multiple_of(zh * 2 * RB, 2 * RB), 2 * RB)

    def out_rows(g):
        start = (g // SPLIT) * 32 + (g % SPLIT) * RB
        return slice(start, start + RB)

    def project(g):
        s, half = g // SPLIT, g % SPLIT
        if s not in gathered:
            gathered.append(s)
            gather_4(heads.at[s], ("heads", s))
        ordered = jnp.concatenate(
            [heads[s, n % 2, (n // 2 % 4) * 2 + n // 8] for n in range(16)], axis=0
        )
        by_request = dot(perm[half * span : (half + 1) * span, :], ordered).astype(BF)
        part[g] = dot_nt(by_request, w_out[...]).astype(BF).reshape(16, RB, 448)
        scatter_1(part.at[g], part_y.at[g], ("out", g))

    def project_2(g):
        scatter_2(part.at[g], part_y.at[g], part_mid.at[g], part_z.at[g], ("out", g))

    def residual(g):
        total = scatter_3(part_mid.at[g], part_z.at[g], ("out", g))
        block_rows = (hidden_ref[out_rows(g), :].astype(F32) + total).astype(BF)
        wide = block_rows.astype(F32)
        square = jnp.sum(wide * wide, axis=1, keepdims=True)
        first = square.astype(BF).astype(F32)
        second = (square - first).astype(BF).astype(F32)
        third = square - first - second
        lane = iota((RB, 64), 1)
        beside = jnp.where(lane == 0, first, jnp.where(lane == 1, second, third))
        x_all[g, c, t, :, 0:448] = block_rows
        x_all[g, c, t, :, 448:512] = beside.astype(BF)
        for k in (2, 1, 3):
            send(x_all.at[g, c, t], x_all.at[g, c, t], ("x", g, "z"), along_z(k))

    def spread_y(g):
        arrived(x_all.at[g, c, pl.ds(0, 3)], ("x", g, "z"))
        for k in (2, 1, 3):
            send(quad(g, y), quad(g, y), ("x", g, "y"), along_y(k))
        send(quad(g, y), quad(g, y), ("x", g, "core"), sibling)

    def spread_core(g):
        arrived(x_all.at[g, c, pl.ds(0, 12)], ("x", g, "y"))
        for k in range(1, 4):
            j = lax.rem(y + k, 4)
            send(quad(g, j), quad(g, j), ("x", g, "core"), sibling)

    def gate_up(g):
        arrived(x_all.at[g, other], ("x", g, "core"))

    def gate_part(g, p):
        rows = [x_all[g, core, :, :, 0:448].reshape(16 * RB, 448) for core in range(2)]
        cols = slice(p * 384, (p + 1) * 384)
        value = dot(rows[0], w_mix[0, :, cols]) + dot(rows[1], w_mix[1, :, cols])
        y_part[g, p] = value.astype(BF).reshape(4, 4 * RB, 384)
        after, before, away = (lax.rem(x + k, 4) for k in (1, 3, 2))
        send(y_part.at[g, p, away, low_rows], y_far.at[g, p, 0], ("gate", g, "far", p), along_x(1))
        send(y_part.at[g, p, away, high_rows], y_far.at[g, p, 1], ("gate", g, "far", p), along_x(3))
        group = ("gate", g, "x", p)
        send(y_part.at[g, p, after, high_rows], y_recv.at[g, p, 0, high_rows], group, along_x(1))
        send(y_part.at[g, p, before, low_rows], y_recv.at[g, p, 1, low_rows], group, along_x(3))

    def pass_on(g, p):
        arrived(y_far.at[g, p], ("gate", g, "far", p))
        after, before = (lax.rem(x + k, 4) for k in (1, 3))
        group = ("gate", g, "x", p)
        total = y_part[g, p, after, low_rows, :].astype(F32) + y_far[g, p, 0].astype(F32)
        y_pass[g, p, 0] = total.astype(BF)
        send(y_pass.at[g, p, 0], y_recv.at[g, p, 0, low_rows], group, along_x(1))
        total = y_part[g, p, before, high_rows, :].astype(F32) + y_far[g, p, 1].astype(F32)
        y_pass[g, p, 1] = total.astype(BF)
        send(y_pass.at[g, p, 1], y_recv.at[g, p, 1, high_rows], group, along_x(3))

    def pass_on_0(g):
        pass_on(g, 0)

    def pass_on_1(g):
        pass_on(g, 1)

    def pass_on_2(g):
        pass_on(g, 2)

    def gate_up_0(g):
        gate_up(g)
        gate_part(g, 0)

    def gate_up_1(g):
        gate_part(g, 1)

    def gate_up_2(g):
        gate_part(g, 2)
        squares = jnp.zeros((8, 16 * RB), F32)
        for core in range(2):
            beside = x_all[g, core, :, :, 384:512].reshape(16 * RB, 128)
            squares = squares + dot_nt(sum_lanes, beside)
        for n in range(8):
            s_part[g, n // 2, n % 2, :, 0 : 2 * RB] = squares[:, n * 2 * RB : (n + 1) * 2 * RB]
        for k in (2, 1, 3):
            j = lax.rem(x + k, 4)
            send(s_part.at[g, j], s_recv.at[g, k - 1], ("gate", g, "xs"), along_x(k))

    def x_sum(g, p, rows):
        total = y_part[g, p, x, rows, :].astype(F32)
        for k in range(2):
            total = total + y_recv[g, p, k, rows, :].astype(F32)
        return total

    def s_sum(g, half):
        total = s_part[g, x, half]
        for k in range(3):
            total = total + s_recv[g, k, half]
        return total

    def gate_z(g, p):
        arrived(y_recv.at[g, p], ("gate", g, "x", p))
        y_mid[g, p] = x_sum(g, p, far_rows).astype(BF)
        send(y_mid.at[g, p], y_last.at[g, p], ("gate", g, "z", p), z_partner)

    def gate_z_0(g):
        gate_z(g, 0)

    def gate_z_1(g):
        gate_z(g, 1)

    def gate_z_2(g):
        gate_z(g, 2)
        arrived(s_recv.at[g], ("gate", g, "xs"))
        s_mid[g] = s_sum(g, 1 - zh)
        send(s_mid.at[g], s_last.at[g], ("gate", g, "zs"), z_partner)

    def activate(g):
        parts = [x_sum(g, p, own_rows) for p in range(3)]
        squares = s_sum(g, zh)
        for p in range(3):
            arrived(y_last.at[g, p], ("gate", g, "z", p))
        arrived(s_last.at[g], ("gate", g, "zs"))
        squares = (squares + s_last[g])[0:1, 0 : 2 * RB]
        inverse = lax.rsqrt(squares * (1.0 / D) + 1e-6)
        diagonal = iota((2 * RB, 2 * RB), 0) == iota((2 * RB, 2 * RB), 1)
        inverse = jnp.sum(jnp.where(diagonal, inverse, 0.0), axis=1, keepdims=True)
        parts = [parts[p] + y_last[g, p].astype(F32) for p in range(3)]
        both = jnp.concatenate(parts, axis=1) * inverse
        acts[g, c, block, :, 0:512] = (silu(both[:, 0:512]) * both[:, 512:1024]).astype(BF)
        tail = both[:, 1024:1152]
        tail = jnp.where(
            iota((2 * RB, 128), 1) < 64, silu(tail) * pltpu.roll(tail, 64, 1), 0.0
        )
        acts[g, c, block, :, 512:640] = jnp.where(c == 0, tail, pltpu.roll(tail, 64, 1)).astype(BF)
        gather_1(acts.at[g], ("act", g))

    def act_x(g):
        gather_2(acts.at[g], ("act", g))

    def act_core(g):
        gather_3(acts.at[g], ("act", g))

    def descend(g):
        gather_4(acts.at[g], ("act", g))
        left = acts[g, 0].reshape(16 * RB, 640)
        right = acts[g, 1].reshape(16 * RB, 640)
        out = dot_nt(left[:, 0:512], w_down[:, 0:512]) + dot_nt(right[:, 0:512], w_down[:, 512:1024])
        out = out + dot_nt(left[:, 512:640] + right[:, 512:640], w_down[:, 1024:1152])
        down_part[g] = out.astype(BF).reshape(16, RB, 448)
        scatter_1(down_part.at[g], down_y.at[g], ("down", g))

    def descend_2(g):
        scatter_2(down_part.at[g], down_y.at[g], down_mid.at[g], down_z.at[g], ("down", g))

    def finish(g):
        if len(order) == 0:
            all_sent()
        fed = scatter_3(down_mid.at[g], down_z.at[g], ("down", g))
        o_ref[out_rows(g), :] = (x_all[g, c, t, :, 0:448].astype(F32) + fed).astype(BF)

    def heads_x(s):
        gather_2(heads.at[s], ("heads", s))

    def heads_core(s):
        gather_3(heads.at[s], ("heads", s))

    stages = [
        project,
        project_2,
        residual,
        spread_y,
        spread_core,
        gate_up_0,
        gate_up_1,
        gate_up_2,
        pass_on_0,
        pass_on_1,
        pass_on_2,
        gate_z_0,
        gate_z_1,
        gate_z_2,
        activate,
        act_x,
        act_core,
        descend,
        descend_2,
        finish,
    ]
    gathered = []
    order = list(ORDER)
    steps = {name: iter((head_outputs, heads_x, heads_core)) for name in "01"}
    steps.update({name: iter(stages) for name in "abcd"[:CHUNKS]})
    while order:
        name = order.pop(0)
        next(steps[name])("01".find(name) if name in "01" else "abcd".find(name))
    all_sent()


def on_device(
    q_nope,
    q_rope,
    cache_latent,
    cache_rope,
    cache_len,
    new_latent,
    new_rope,
    slot_request,
    w_uk,
    w_uv,
    w_out,
    hidden_state,
    norm_gain,
    w_gate,
    w_up,
    w_down,
):
    vmem = pl.BlockSpec(memory_space=pltpu.VMEM)
    anywhere = pl.BlockSpec(memory_space=pl.ANY)

    def buf(*shape, dtype=BF):
        return pltpu.VMEM(shape, dtype)

    out = pl.pallas_call(
        layer_kernel,
        out_shape=pltpu.VMEM((64, 448), BF),
        in_specs=[pl.BlockSpec(memory_space=pltpu.SMEM), vmem, vmem] + [anywhere] * 13,
        out_specs=vmem,
        scratch_shapes=[
            buf(2, 2, 512),
            buf(2, 2, 64),
            buf(64, 448),
            buf(2, 2, 64, 128),
            buf(2, 2, 64, 64),
            buf(16, 16, 128),
            buf(16, 16, 128),
            buf(2, 16, 16, 256),
            buf(2, 16, 16, 256),
            buf(2, 16, 16, 256),
            buf(2, 16, 16, 256),
            buf(2, 2048, 512),
            buf(2, 64, 2048),
            buf(4, 128, 512),
            buf(4, 512, 128),
            buf(448, 512),
            buf(448, 1152),
            buf(2, 448, 1280),
            buf(2, 448, 1152),
            buf(2, 8, 448, dtype=F32),
            buf(512, 512),
            buf(256, 256),
            buf(2, 256, 256),
            buf(2, 128, 256),
            buf(2, 256, 128),
            buf(32, 128),
            buf(2, 2, 8, 32, 512),
            buf(CHUNKS, 16, RB, 448),
            buf(CHUNKS, 3, 4, RB, 448),
            buf(CHUNKS, 4, RB, 448),
            buf(CHUNKS, 3, RB, 448),
            buf(CHUNKS, 2, 16, RB, 512),
            buf(CHUNKS, 3, 4, 4 * RB, 384),
            buf(CHUNKS, 3, 2, 4 * RB, 384),
            buf(CHUNKS, 3, 2, 2 * RB, 384),
            buf(CHUNKS, 3, 2, 2 * RB, 384),
            buf(CHUNKS, 4, 2, 8, 128, dtype=F32),
            buf(CHUNKS, 3, 2, 8, 128, dtype=F32),
            buf(CHUNKS, 3, 2 * RB, 384),
            buf(CHUNKS, 3, 2 * RB, 384),
            buf(CHUNKS, 8, 128, dtype=F32),
            buf(CHUNKS, 8, 128, dtype=F32),
            buf(CHUNKS, 2, 8, 2 * RB, 640),
            buf(CHUNKS, 16, RB, 448),
            buf(CHUNKS, 3, 4, RB, 448),
            buf(CHUNKS, 4, RB, 448),
            buf(CHUNKS, 3, RB, 448),
            pltpu.SemaphoreType.DMA((15,)),
            pltpu.SemaphoreType.DMA((18 + 22 * CHUNKS,)),
            pltpu.SemaphoreType.DMA((18 + 22 * CHUNKS,)),
        ],
        compiler_params=pltpu.CompilerParams(
            collective_id=0, has_side_effects=True, vmem_limit_bytes=56 * 1024 * 1024
        ),
        name="layer",
    )(
        cache_len,
        slot_request.reshape(1, 512),
        norm_gain,
        new_latent,
        new_rope,
        hidden_state.reshape(64, 448),
        q_nope,
        q_rope,
        cache_latent,
        cache_rope,
        w_uk,
        w_uv,
        w_out.T,
        w_gate,
        w_up,
        w_down.T,
    )
    return out.reshape(2, 32, 448)


def solution(mesh):
    return jax.shard_map(
        on_device,
        mesh=mesh,
        in_specs=(
            P(None, ("dp", "tensor"), None, None),
            P(None, ("dp", "tensor"), None, None),
            P(("dp", "tensor"), None, None),
            P(("dp", "tensor"), None, None),
            P(("dp", "tensor")),
            P(None, ("dp", "tensor"), None),
            P(None, ("dp", "tensor"), None),
            P(),
            P("tensor", None, None),
            P("tensor", None, None),
            P("tensor", "dp"),
            P(None, "tensor", "dp"),
            P("dp"),
            P("dp", "tensor"),
            P("dp", "tensor"),
            P("tensor", "dp"),
        ),
        out_specs=P(None, "tensor", "dp"),
        check_vma=False,
    )
```

```python
import jax
import jax.numpy as jnp
from jax import lax
from jax.experimental import pallas as pl
from jax.experimental.pallas import tpu as pltpu
from jax.sharding import PartitionSpec as P

D = 7168
MESH = pl.DeviceIdType.MESH
BF = jnp.bfloat16
F32 = jnp.float32


def dot(a, b):
    return jnp.dot(a, b, preferred_element_type=F32)


def dot_nt(a, b):
    return lax.dot_general(a, b, (((1,), (1,)), ((), ())), preferred_element_type=F32)


def iota(shape, dim):
    return lax.broadcasted_iota(jnp.int32, shape, dim)


CHUNKS = 4
SPLIT = CHUNKS // 2
RB = 32 // SPLIT
SENDS = 40
ORDER = "".join(
    (
        "0010b1a1bdacbdabcdabcbdb",
        "bacbabadbaadbbcadabdadca",
        "cdadcdbcddccacbccdbacadb",
        "acddcacbdcbdac",
    )
)


def layer_kernel(
    len_ref,
    slot_ref,
    gain_ref,
    new_lat_hbm,
    new_rot_hbm,
    hidden_hbm,
    q_hbm,
    q_rot_hbm,
    lat_hbm,
    rot_hbm,
    uk_hbm,
    uv_hbm,
    out_hbm,
    gate_hbm,
    up_hbm,
    down_hbm,
    o_ref,
    new_lat_ref,
    new_rot_ref,
    hidden_ref,
    q_raw,
    q_rot_raw,
    q_send,
    q_recv,
    ql_send,
    ql_recv,
    ol_send,
    ol_recv,
    lat,
    rot,
    uk,
    uv,
    w_out,
    w_down,
    w_in,
    w_mix,
    gains,
    perm,
    by_block,
    picks,
    to_slots,
    to_blocks,
    pick,
    heads,
    part,
    part_y,
    part_mid,
    part_z,
    x_all,
    y_part,
    y_recv,
    y_far,
    y_pass,
    s_part,
    s_recv,
    y_mid,
    y_last,
    s_mid,
    s_last,
    acts,
    down_part,
    down_y,
    down_mid,
    down_z,
    local_sem,
    send_sem,
    recv_sem,
):
    d = lax.axis_index("dp")
    t = lax.axis_index("tensor")
    zh = lax.div(d, 8)
    x = lax.rem(lax.div(d, 2), 4)
    c = lax.rem(d, 2)
    y = lax.div(t, 4)
    zl = lax.rem(t, 4)
    other = 1 - c
    sibling = (d + 1 - 2 * c, t)
    z_partner = (lax.rem(d + 8, 16), t)
    block = x * 2 + zh
    far = x * 2 + 1 - zh

    def along_x(k):
        return (zh * 8 + lax.rem(x + k + 4, 4) * 2 + c, t)

    def along_y(k):
        return (d, lax.rem(y + k + 4, 4) * 4 + zl)

    def along_z(k):
        return (d, y * 4 + lax.rem(zl + k + 4, 4))

    sent = []
    groups = {}
    in_use = {}
    spare = list(range(SENDS))

    def remote(src, dst, group, device):
        n = groups.setdefault(group, len(groups))
        if group not in in_use:
            in_use[group] = spare.pop(0)
        return pltpu.make_async_remote_copy(
            src_ref=src,
            dst_ref=dst,
            send_sem=send_sem.at[in_use[group]],
            recv_sem=recv_sem.at[n],
            device_id=device,
            device_id_type=MESH,
        )

    def send(src, dst, group, device):
        remote(src, dst, group, device).start()

    def arrived(whole, group):
        remote(whole, whole, group, sibling).wait_recv()
        sent.append((group, remote(whole, whole, group, sibling)))
        if len(sent) > 8:
            oldest_sent()

    def oldest_sent():
        group, copy = sent.pop(0)
        copy.wait_send()
        spare.append(in_use[group])

    def all_sent():
        while sent:
            oldest_sent()

    def one_hot(ref, mask):
        ref[...] = jnp.where(mask, 1.0, 0.0).astype(BF)

    def load(src, dst, i):
        copy = pltpu.make_async_copy(src, dst, local_sem.at[i])
        copy.start()
        return copy

    barrier = pltpu.get_barrier_semaphore()
    for device in (z_partner, along_x(2), along_x(1), along_x(3), sibling):
        pl.semaphore_signal(barrier, inc=1, device_id=device, device_id_type=MESH)

    def greet(i, carry):
        pl.semaphore_signal(
            barrier, inc=1, device_id=(d, lax.rem(t + i, 16)), device_id_type=MESH
        )
        return carry

    lax.fori_loop(1, 16, greet, 0)

    load_q = load(q_hbm, q_raw, 0)
    load_uk = load(uk_hbm, uk, 1)
    load_q_rot = load(q_rot_hbm, q_rot_raw, 2)
    mine = pl.ds(pl.multiple_of(c * 512, 512), 512)
    load_in = [
        load(gate_hbm.at[:, mine], w_in.at[c, :, pl.ds(0, 512)], 3),
        load(up_hbm.at[:, mine], w_in.at[c, :, pl.ds(512, 512)], 4),
        load(gate_hbm.at[:, pl.ds(1024, 128)], w_in.at[c, :, pl.ds(1024, 128)], 5),
        load(up_hbm.at[:, pl.ds(1024, 128)], w_in.at[c, :, pl.ds(1152, 128)], 6),
    ]
    load_small = [
        load(new_lat_hbm, new_lat_ref, 12),
        load(new_rot_hbm, new_rot_ref, 13),
        load(hidden_hbm, hidden_ref, 14),
    ]
    load_lat = load(lat_hbm, lat, 7)
    load_rot = load(rot_hbm, rot, 8)
    load_uv = load(uv_hbm, uv, 9)
    load_out = load(out_hbm, w_out, 10)
    load_down = load(down_hbm, w_down, 11)

    row = iota((256, 256), 0)
    col = iota((256, 256), 1)
    source = ((row & 8) << 4) + ((row & 4) << 4) + ((row >> 4) << 2) + (row & 3)
    one_hot(by_block, col == source)
    for s in range(2):
        one_hot(picks.at[s], col == ((row >> 4) << 4) + 8 * s + (row & 7))
    def position(m, half):
        return ((m & 60) << 2) + half * 8 + ((m >> 6) << 2) + (m & 3)

    for half in range(2):
        one_hot(to_slots.at[half], iota((128, 256), 1) == position(iota((128, 256), 0), half))
        one_hot(to_blocks.at[half], iota((256, 128), 0) == position(iota((256, 128), 1), half))
    col = iota((32, 128), 1)
    one_hot(pick, (((col & 60) >> 1) + (col >> 6)) == iota((32, 128), 0))
    row = iota((512, 512), 0)
    span = 512 // SPLIT
    if SPLIT == 1:
        request = row
    else:
        request = ((row & 255) >> 4 << 5) + (row >> 8 << 4) + (row & 15)
    one_hot(perm, request == slot_ref[...])
    load_q.wait()
    q_send[...] = dot(by_block[...], q_raw[...].reshape(256, 128)).astype(BF).reshape(16, 16, 128)
    gains[c] = jnp.broadcast_to(gain_ref[...].astype(F32).reshape(1, 448), (8, 448))
    pl.semaphore_wait(barrier, 20)

    def exchange_start(src, dst, group):
        def one(i, carry):
            p = lax.rem(t + i, 16)
            send(src.at[p], dst.at[t], group, (d, p))
            return carry

        lax.fori_loop(1, 16, one, 0)
        dst[t] = src[t]

    def exchange_wait(dst, group):
        arrived(dst.at[pl.ds(0, 15)], group)

    exchange_start(q_send, q_recv, "q")

    theirs = pl.ds(pl.multiple_of(other * 512, 512), 512)
    send(gains.at[c], gains.at[c], ("w", 4), sibling)
    send(gate_hbm.at[:, theirs], w_in.at[c, :, pl.ds(0, 512)], ("w", 0), sibling)
    send(up_hbm.at[:, theirs], w_in.at[c, :, pl.ds(512, 512)], ("w", 1), sibling)
    send(gate_hbm.at[:, pl.ds(1024, 128)], w_in.at[c, :, pl.ds(1024, 128)], ("w", 2), sibling)
    send(up_hbm.at[:, pl.ds(1024, 128)], w_in.at[c, :, pl.ds(1152, 128)], ("w", 3), sibling)

    head_of_row = iota((256, 512), 0) & 3
    first_half = (iota((256, 256), 0) & 8) == 0
    load_uk.wait()
    exchange_wait(q_recv, "q")
    q_all = q_recv[...].reshape(256, 128)
    for s in range(2):
        q_rows = dot(picks[s], q_all).astype(BF)
        q_lat = jnp.zeros((256, 512), F32)
        for j in range(4):
            q_lat = jnp.where(head_of_row == j, dot(q_rows, uk[j]), q_lat)
        q_lat = jnp.where(first_half, q_lat[:, 0:256], q_lat[:, 256:512])
        ql_send[s] = q_lat.astype(BF).reshape(16, 16, 256)
        exchange_start(ql_send.at[s], ql_recv.at[s], ("ql", s))

    def slot_rows(blocks):
        blocks = blocks.reshape(256, 256)
        return jnp.concatenate([dot(to_slots[0], blocks), dot(to_slots[1], blocks)], axis=1)

    load_q_rot.wait()
    for copy in load_small:
        copy.wait()
    load_lat.wait()
    load_rot.wait()
    scale = 1.0 / 192.0**0.5
    for s in range(2):
        exchange_wait(ql_recv.at[s], ("ql", s))
        q_rows = slot_rows(ql_recv[s])
        results = []
        for r in range(2):
            q_wide = q_rows[64 * r : 64 * r + 64, :]
            q_turned = q_rot_raw[s, r]
            scores = (dot_nt(q_wide.astype(BF), lat[r]) + dot(q_turned, rot[r])) * scale
            scores = jnp.where(iota((64, 2048), 1) < len_ref[r], scores, -1e30)
            q_turned_wide = q_turned.astype(F32)
            top = jnp.max(scores, axis=1, keepdims=True)
            fresh = []
            for u in range(s + 1):
                value = jnp.sum(
                    q_wide * new_lat_ref[u, r : r + 1, :].astype(F32), axis=1, keepdims=True
                )
                value = value + jnp.sum(
                    q_turned_wide * new_rot_ref[u, r : r + 1, :].astype(F32), axis=1, keepdims=True
                )
                value = value * scale
                top = jnp.maximum(top, value)
                fresh.append(value)
            weights = jnp.exp(scores - top)
            total = jnp.sum(weights, axis=1, keepdims=True)
            mixed = dot(weights.astype(BF), lat[r])
            for u in range(s + 1):
                weight = jnp.exp(fresh[u] - top)
                total = total + weight
                mixed = mixed + weight * new_lat_ref[u, r : r + 1, :].astype(F32)
            results.append((mixed / total).astype(BF))
        mixed = jnp.concatenate(results, axis=0)
        mixed = dot(to_blocks[0], mixed[:, 0:256]) + dot(to_blocks[1], mixed[:, 256:512])
        ol_send[s] = mixed.astype(BF).reshape(16, 16, 256)
        exchange_start(ol_send.at[s], ol_recv.at[s], ("ol", s))

    for copy in load_in:
        copy.wait()
    arrived(w_in.at[other, :, pl.ds(0, 512)], ("w", 0))
    arrived(w_in.at[other, :, pl.ds(512, 512)], ("w", 1))
    arrived(w_in.at[other, :, pl.ds(1024, 128)], ("w", 2))
    arrived(w_in.at[other, :, pl.ds(1152, 128)], ("w", 3))
    arrived(gains.at[other], ("w", 4))
    low = iota((448, 128), 1) < 64
    eye = iota((448, 448), 0) == iota((448, 448), 1)
    for k in range(2):
        gain = jnp.sum(jnp.where(eye, gains[k, 0:1, :], 0.0), axis=1, keepdims=True)
        for j in range(8):
            cols = pl.ds(j * 128, 128)
            w_mix[k, :, cols] = (w_in[k, :, cols].astype(F32) * gain).astype(BF)
        gate_tail = w_in[k, :, pl.ds(1024, 128)].astype(F32)
        up_tail = w_in[k, :, pl.ds(1152, 128)].astype(F32)
        first = jnp.where(low, gate_tail, pltpu.roll(up_tail, 64, 1))
        second = jnp.where(low, pltpu.roll(gate_tail, 64, 1), up_tail)
        tail = jnp.where(c == 0, first, second)
        w_mix[k, :, pl.ds(1024, 128)] = (tail * gain).astype(BF)

    load_uv.wait()
    load_out.wait()
    load_down.wait()
    own_head = iota((128, 128), 0) & 3

    def head_outputs(s):
        exchange_wait(ol_recv.at[s], ("ol", s))
        o_rows = slot_rows(ol_recv[s]).astype(BF)
        spread = [jnp.where(own_head == j, dot(o_rows, uv[j]), 0.0).astype(BF) for j in range(4)]
        heads[s, c, block] = dot(pick[...], jnp.concatenate(spread, axis=1)).astype(BF)
        gather_1(heads.at[s], ("heads", s))

    def gather_send(buf, b, group):
        for k in (2, 1, 3):
            send(buf.at[c, b], buf.at[c, b], group, along_x(k))

    def gather_1(buf, group):
        send(buf.at[c, block], buf.at[c, block], group + ("z",), z_partner)
        gather_send(buf, block, group + ("x",))

    def pair(buf, j):
        return buf.at[c, pl.ds(2 * j, 2)]

    def gather_2(buf, group):
        arrived(buf.at[c, far], group + ("z",))
        gather_send(buf, far, group + ("xz",))
        send(pair(buf, x), pair(buf, x), group + ("core",), sibling)

    def gather_3(buf, group):
        arrived(buf.at[c, pl.ds(0, 3)], group + ("x",))
        arrived(buf.at[c, pl.ds(0, 3)], group + ("xz",))
        for k in range(1, 4):
            j = lax.rem(x + k, 4)
            send(pair(buf, j), pair(buf, j), group + ("core",), sibling)

    def gather_4(buf, group):
        arrived(buf.at[other], group + ("core",))

    def scatter_1(buf, from_y, group):
        for k in (2, 1, 3):
            j = lax.rem(y + k, 4)
            send(buf.at[pl.ds(4 * j, 4)], from_y.at[k - 1], group + ("y",), along_y(k))

    def scatter_2(buf, from_y, mid, from_z, group):
        total = buf[pl.ds(4 * y, 4)].astype(F32)
        arrived(from_y, group + ("y",))
        for k in range(3):
            total = total + from_y[k].astype(F32)
        mid[...] = total.astype(BF)
        for k in (2, 1, 3):
            send(mid.at[lax.rem(zl + k, 4)], from_z.at[k - 1], group + ("z",), along_z(k))

    def scatter_3(mid, from_z, group):
        total = mid[zl].astype(F32)
        arrived(from_z, group + ("z",))
        for k in range(3):
            total = total + from_z[k].astype(F32)
        return total

    def quad(g, j):
        return x_all.at[g, c, pl.ds(4 * j, 4)]

    def silu(v):
        return v / (1.0 + jnp.exp(-v))

    lane = iota((8, 128), 1)
    sum_lanes = jnp.where((lane >= 64) & (lane < 67), 1.0, 0.0).astype(BF)
    low_rows = pl.ds(0, 2 * RB)
    high_rows = pl.ds(2 * RB, 2 * RB)
    far_rows = pl.ds(pl.multiple_of((1 - zh) * 2 * RB, 2 * RB), 2 * RB)
    own_rows = pl.ds(pl.multiple_of(zh * 2 * RB, 2 * RB), 2 * RB)

    def out_rows(g):
        start = (g // SPLIT) * 32 + (g % SPLIT) * RB
        return slice(start, start + RB)

    def project(g):
        s, half = g // SPLIT, g % SPLIT
        if s not in gathered:
            gathered.append(s)
            gather_4(heads.at[s], ("heads", s))
        ordered = jnp.concatenate(
            [heads[s, n % 2, (n // 2 % 4) * 2 + n // 8] for n in range(16)], axis=0
        )
        by_request = dot(perm[half * span : (half + 1) * span, :], ordered).astype(BF)
        part[g] = dot_nt(by_request, w_out[...]).astype(BF).reshape(16, RB, 448)
        scatter_1(part.at[g], part_y.at[g], ("out", g))

    def project_2(g):
        scatter_2(part.at[g], part_y.at[g], part_mid.at[g], part_z.at[g], ("out", g))

    def residual(g):
        total = scatter_3(part_mid.at[g], part_z.at[g], ("out", g))
        block_rows = (hidden_ref[out_rows(g), :].astype(F32) + total).astype(BF)
        wide = block_rows.astype(F32)
        square = jnp.sum(wide * wide, axis=1, keepdims=True)
        first = square.astype(BF).astype(F32)
        second = (square - first).astype(BF).astype(F32)
        third = square - first - second
        lane = iota((RB, 64), 1)
        beside = jnp.where(lane == 0, first, jnp.where(lane == 1, second, third))
        x_all[g, c, t, :, 0:448] = block_rows
        x_all[g, c, t, :, 448:512] = beside.astype(BF)
        for k in (2, 1, 3):
            send(x_all.at[g, c, t], x_all.at[g, c, t], ("x", g, "z"), along_z(k))

    def spread_y(g):
        arrived(x_all.at[g, c, pl.ds(0, 3)], ("x", g, "z"))
        for k in (2, 1, 3):
            send(quad(g, y), quad(g, y), ("x", g, "y"), along_y(k))
        send(quad(g, y), quad(g, y), ("x", g, "core"), sibling)

    def spread_core(g):
        arrived(x_all.at[g, c, pl.ds(0, 12)], ("x", g, "y"))
        for k in range(1, 4):
            j = lax.rem(y + k, 4)
            send(quad(g, j), quad(g, j), ("x", g, "core"), sibling)

    def gate_up(g):
        arrived(x_all.at[g, other], ("x", g, "core"))

    def gate_part(g, p):
        rows = [x_all[g, core, :, :, 0:448].reshape(16 * RB, 448) for core in range(2)]
        cols = slice(p * 384, (p + 1) * 384)
        value = dot(rows[0], w_mix[0, :, cols]) + dot(rows[1], w_mix[1, :, cols])
        y_part[g, p] = value.astype(BF).reshape(4, 4 * RB, 384)
        after, before, away = (lax.rem(x + k, 4) for k in (1, 3, 2))
        send(y_part.at[g, p, away, low_rows], y_far.at[g, p, 0], ("gate", g, "far", p), along_x(1))
        send(y_part.at[g, p, away, high_rows], y_far.at[g, p, 1], ("gate", g, "far", p), along_x(3))
        group = ("gate", g, "x", p)
        send(y_part.at[g, p, after, high_rows], y_recv.at[g, p, 0, high_rows], group, along_x(1))
        send(y_part.at[g, p, before, low_rows], y_recv.at[g, p, 1, low_rows], group, along_x(3))

    def pass_on(g, p):
        arrived(y_far.at[g, p], ("gate", g, "far", p))
        after, before = (lax.rem(x + k, 4) for k in (1, 3))
        group = ("gate", g, "x", p)
        total = y_part[g, p, after, low_rows, :].astype(F32) + y_far[g, p, 0].astype(F32)
        y_pass[g, p, 0] = total.astype(BF)
        send(y_pass.at[g, p, 0], y_recv.at[g, p, 0, low_rows], group, along_x(1))
        total = y_part[g, p, before, high_rows, :].astype(F32) + y_far[g, p, 1].astype(F32)
        y_pass[g, p, 1] = total.astype(BF)
        send(y_pass.at[g, p, 1], y_recv.at[g, p, 1, high_rows], group, along_x(3))

    def pass_on_0(g):
        pass_on(g, 0)

    def pass_on_1(g):
        pass_on(g, 1)

    def pass_on_2(g):
        pass_on(g, 2)

    def gate_up_0(g):
        gate_up(g)
        gate_part(g, 0)

    def gate_up_1(g):
        gate_part(g, 1)

    def gate_up_2(g):
        gate_part(g, 2)
        squares = jnp.zeros((8, 16 * RB), F32)
        for core in range(2):
            beside = x_all[g, core, :, :, 384:512].reshape(16 * RB, 128)
            squares = squares + dot_nt(sum_lanes, beside)
        for n in range(8):
            s_part[g, n // 2, n % 2, :, 0 : 2 * RB] = squares[:, n * 2 * RB : (n + 1) * 2 * RB]
        for k in (2, 1, 3):
            j = lax.rem(x + k, 4)
            send(s_part.at[g, j], s_recv.at[g, k - 1], ("gate", g, "xs"), along_x(k))

    def x_sum(g, p, rows):
        total = y_part[g, p, x, rows, :].astype(F32)
        for k in range(2):
            total = total + y_recv[g, p, k, rows, :].astype(F32)
        return total

    def s_sum(g, half):
        total = s_part[g, x, half]
        for k in range(3):
            total = total + s_recv[g, k, half]
        return total

    def gate_z(g, p):
        arrived(y_recv.at[g, p], ("gate", g, "x", p))
        y_mid[g, p] = x_sum(g, p, far_rows).astype(BF)
        send(y_mid.at[g, p], y_last.at[g, p], ("gate", g, "z", p), z_partner)

    def gate_z_0(g):
        gate_z(g, 0)

    def gate_z_1(g):
        gate_z(g, 1)

    def gate_z_2(g):
        gate_z(g, 2)
        arrived(s_recv.at[g], ("gate", g, "xs"))
        s_mid[g] = s_sum(g, 1 - zh)
        send(s_mid.at[g], s_last.at[g], ("gate", g, "zs"), z_partner)

    def activate(g):
        parts = [x_sum(g, p, own_rows) for p in range(3)]
        squares = s_sum(g, zh)
        for p in range(3):
            arrived(y_last.at[g, p], ("gate", g, "z", p))
        arrived(s_last.at[g], ("gate", g, "zs"))
        squares = (squares + s_last[g])[0:1, 0 : 2 * RB]
        inverse = lax.rsqrt(squares * (1.0 / D) + 1e-6)
        diagonal = iota((2 * RB, 2 * RB), 0) == iota((2 * RB, 2 * RB), 1)
        inverse = jnp.sum(jnp.where(diagonal, inverse, 0.0), axis=1, keepdims=True)
        parts = [parts[p] + y_last[g, p].astype(F32) for p in range(3)]
        both = jnp.concatenate(parts, axis=1) * inverse
        acts[g, c, block, :, 0:512] = (silu(both[:, 0:512]) * both[:, 512:1024]).astype(BF)
        tail = both[:, 1024:1152]
        tail = jnp.where(
            iota((2 * RB, 128), 1) < 64, silu(tail) * pltpu.roll(tail, 64, 1), 0.0
        )
        acts[g, c, block, :, 512:640] = jnp.where(c == 0, tail, pltpu.roll(tail, 64, 1)).astype(BF)
        gather_1(acts.at[g], ("act", g))

    def act_x(g):
        gather_2(acts.at[g], ("act", g))

    def act_core(g):
        gather_3(acts.at[g], ("act", g))

    def descend(g):
        gather_4(acts.at[g], ("act", g))
        left = acts[g, 0].reshape(16 * RB, 640)
        right = acts[g, 1].reshape(16 * RB, 640)
        out = dot_nt(left[:, 0:512], w_down[:, 0:512]) + dot_nt(right[:, 0:512], w_down[:, 512:1024])
        out = out + dot_nt(left[:, 512:640] + right[:, 512:640], w_down[:, 1024:1152])
        down_part[g] = out.astype(BF).reshape(16, RB, 448)
        scatter_1(down_part.at[g], down_y.at[g], ("down", g))

    def descend_2(g):
        scatter_2(down_part.at[g], down_y.at[g], down_mid.at[g], down_z.at[g], ("down", g))

    def finish(g):
        if len(order) == 0:
            all_sent()
        fed = scatter_3(down_mid.at[g], down_z.at[g], ("down", g))
        o_ref[out_rows(g), :] = (x_all[g, c, t, :, 0:448].astype(F32) + fed).astype(BF)

    def heads_x(s):
        gather_2(heads.at[s], ("heads", s))

    def heads_core(s):
        gather_3(heads.at[s], ("heads", s))

    stages = [
        project,
        project_2,
        residual,
        spread_y,
        spread_core,
        gate_up_0,
        gate_up_1,
        gate_up_2,
        pass_on_0,
        pass_on_1,
        pass_on_2,
        gate_z_0,
        gate_z_1,
        gate_z_2,
        activate,
        act_x,
        act_core,
        descend,
        descend_2,
        finish,
    ]
    gathered = []
    order = list(ORDER)
    steps = {name: iter((head_outputs, heads_x, heads_core)) for name in "01"}
    steps.update({name: iter(stages) for name in "abcd"[:CHUNKS]})
    while order:
        name = order.pop(0)
        next(steps[name])("01".find(name) if name in "01" else "abcd".find(name))
    all_sent()


def on_device(
    q_nope,
    q_rope,
    cache_latent,
    cache_rope,
    cache_len,
    new_latent,
    new_rope,
    slot_request,
    w_uk,
    w_uv,
    w_out,
    hidden_state,
    norm_gain,
    w_gate,
    w_up,
    w_down,
):
    vmem = pl.BlockSpec(memory_space=pltpu.VMEM)
    anywhere = pl.BlockSpec(memory_space=pl.ANY)

    def buf(*shape, dtype=BF):
        return pltpu.VMEM(shape, dtype)

    out = pl.pallas_call(
        layer_kernel,
        out_shape=pltpu.VMEM((64, 448), BF),
        in_specs=[pl.BlockSpec(memory_space=pltpu.SMEM), vmem, vmem] + [anywhere] * 13,
        out_specs=vmem,
        scratch_shapes=[
            buf(2, 2, 512),
            buf(2, 2, 64),
            buf(64, 448),
            buf(2, 2, 64, 128),
            buf(2, 2, 64, 64),
            buf(16, 16, 128),
            buf(16, 16, 128),
            buf(2, 16, 16, 256),
            buf(2, 16, 16, 256),
            buf(2, 16, 16, 256),
            buf(2, 16, 16, 256),
            buf(2, 2048, 512),
            buf(2, 64, 2048),
            buf(4, 128, 512),
            buf(4, 512, 128),
            buf(448, 512),
            buf(448, 1152),
            buf(2, 448, 1280),
            buf(2, 448, 1152),
            buf(2, 8, 448, dtype=F32),
            buf(512, 512),
            buf(256, 256),
            buf(2, 256, 256),
            buf(2, 128, 256),
            buf(2, 256, 128),
            buf(32, 128),
            buf(2, 2, 8, 32, 512),
            buf(CHUNKS, 16, RB, 448),
            buf(CHUNKS, 3, 4, RB, 448),
            buf(CHUNKS, 4, RB, 448),
            buf(CHUNKS, 3, RB, 448),
            buf(CHUNKS, 2, 16, RB, 512),
            buf(CHUNKS, 3, 4, 4 * RB, 384),
            buf(CHUNKS, 3, 2, 4 * RB, 384),
            buf(CHUNKS, 3, 2, 2 * RB, 384),
            buf(CHUNKS, 3, 2, 2 * RB, 384),
            buf(CHUNKS, 4, 2, 8, 128, dtype=F32),
            buf(CHUNKS, 3, 2, 8, 128, dtype=F32),
            buf(CHUNKS, 3, 2 * RB, 384),
            buf(CHUNKS, 3, 2 * RB, 384),
            buf(CHUNKS, 8, 128, dtype=F32),
            buf(CHUNKS, 8, 128, dtype=F32),
            buf(CHUNKS, 2, 8, 2 * RB, 640),
            buf(CHUNKS, 16, RB, 448),
            buf(CHUNKS, 3, 4, RB, 448),
            buf(CHUNKS, 4, RB, 448),
            buf(CHUNKS, 3, RB, 448),
            pltpu.SemaphoreType.DMA((15,)),
            pltpu.SemaphoreType.DMA((SENDS,)),
            pltpu.SemaphoreType.DMA((18 + 22 * CHUNKS,)),
        ],
        compiler_params=pltpu.CompilerParams(
            collective_id=0, has_side_effects=True, vmem_limit_bytes=56 * 1024 * 1024
        ),
        name="layer",
    )(
        cache_len,
        slot_request.reshape(1, 512),
        norm_gain,
        new_latent,
        new_rope,
        hidden_state.reshape(64, 448),
        q_nope,
        q_rope,
        cache_latent,
        cache_rope,
        w_uk,
        w_uv,
        w_out.T,
        w_gate,
        w_up,
        w_down.T,
    )
    return out.reshape(2, 32, 448)


def solution(mesh):
    return jax.shard_map(
        on_device,
        mesh=mesh,
        in_specs=(
            P(None, ("dp", "tensor"), None, None),
            P(None, ("dp", "tensor"), None, None),
            P(("dp", "tensor"), None, None),
            P(("dp", "tensor"), None, None),
            P(("dp", "tensor")),
            P(None, ("dp", "tensor"), None),
            P(None, ("dp", "tensor"), None),
            P(),
            P("tensor", None, None),
            P("tensor", None, None),
            P("tensor", "dp"),
            P(None, "tensor", "dp"),
            P("dp"),
            P("dp", "tensor"),
            P("dp", "tensor"),
            P("tensor", "dp"),
        ),
        out_specs=P(None, "tensor", "dp"),
        check_vma=False,
    )
```
